512 devices in a mesh: rows: 64 (over z, y), cols: 8 (over x, core).
Axes of the slice: x: 4, y: 8, z: 8, core: 2. Of those that a mesh axis runs over, the one named last changes fastest.
Arguments:
- grads: float32 [131072, 1024], P(('rows', 'cols')), may hold values from -6 to 6
- owners: int32 [131072, 1], P(('rows', 'cols')), may hold values from 0 to 63; in each aligned block of 256 rows (0 to 255, 256 to 511, ...) at most 8 rows name the same one
- local_ids: int32 [131072], P(('rows', 'cols')), may hold values from 0 to 1023
- params: float32 [65536, 1024], P('rows', 'cols'), may hold values from -6 to 6
- first_moment: float32 [65536, 1024], P('rows', 'cols'), may hold values from -4 to 4
- second_moment: float32 [65536, 1024], P('rows', 'cols'), may hold values from 0.0001 to 0.01
- step_count: int32 [1], replicated, may hold values from 1 to 29
Outputs:
- new_params: float32 [65536, 1024], P('rows', 'cols')
- new_first: float32 [65536, 1024], P('rows', 'cols')
- new_second: float32 [65536, 1024], P('rows', 'cols')
- row_steps: bfloat16 [131072, 1024], P(('rows', 'cols'))
The draws below stay inside these ranges and needn't reach their ends.
Inputs may be any that keep to these rules, and one draw needn't show every extreme that they name: `owners`: among the rows of one device, at most 8 name the same owner, a bound that some block reaches of them.
All inputs are finite; a program needn't handle non-finite values.
Results may differ from the reference program's by a relative error of at most 0.001.
Values may be sent and summed in bfloat16 or wider, within the bound.
No kernel may reach another device: no remote copies, remote signals or barrier semaphores. Data moves between devices by JAX's collectives and lax.ppermute only.
A program may use at most 64 MiB of HBM per device.

```python
import math
import jax
import jax.numpy as jnp
import numpy as np

D = 1024
G_DEV = 256
OWN = 1024
CAP = 8
ITEMS = 65536
TOTAL_ROWS = 131072
N_ROWS = 64


def with_ends(values, rng, least, top_value):
    longest = values.shape.index(max(values.shape))
    spots = []
    for shift in (0, 1):
        where = [jax.random.randint(jax.random.fold_in(rng, axis), (), 0, length) for axis, length in enumerate(values.shape)]
        where[longest] = (where[longest] + shift) % values.shape[longest]
        spots.append(tuple(where))
    return values.at[spots[0]].set(least).at[spots[1]].set(top_value)


def level_of(key, shape, split, smallest, top_value):
    loudness = 1.0
    for axis_at, shards_of in split:
        draws = jax.random.uniform(jax.random.fold_in(jax.random.fold_in(key, 6), axis_at), (shards_of,), jnp.float32, smallest / len(split), top_value / len(split))
        loudness = loudness * jnp.repeat(jnp.exp(draws), shape[axis_at] // shards_of).reshape((-1,) + (1,) * (len(shape) - 1 - axis_at))
    return loudness


def cumulative_ranks(amount, lean):
    portions = [(1 << 20) // math.isqrt(rank ** lean) + 1 for rank in range(1, amount + 1)]
    scale = 1 + sum(portions) // (1 << 30)
    return np.cumsum(np.array([max(1, weight // scale) for weight in portions]))


def skewed_ids(rng, shape, count, slope):
    table = cumulative_ranks(count, slope)
    lot = jax.random.randint(jax.random.fold_in(rng, 1), shape, 0, int(table[count - 1]))
    standing = jnp.searchsorted(jnp.asarray(table, jnp.int32), lot, side="right")
    return jax.random.permutation(jax.random.fold_in(rng, 2), count)[standing].astype(jnp.int32)


def shared_out(own_key, own, number, rows, count, top, reach, lean):
    ranking = jax.random.permutation(own_key, count)
    heavy_load, ordinary = load_shares(count, rows * top, reach, lean, True), load_shares(count, rows * top, reach, lean, False)
    places = jnp.arange(count)

    def named(sizes, turn):
        used = int((sizes > 0).sum())
        fixed = max(1, used // 4)
        shifted = fixed + (places - fixed + turn * (used - fixed)) % max(1, count - fixed)
        return jnp.zeros((count,), jnp.int32).at[ranking[jnp.where(places < fixed, places, shifted)]].set(jnp.asarray(sizes, jnp.int32))

    sizes = jnp.where(number % 4 == 0, named(heavy_load, number // 4), named(ordinary, number - number // 4 - 1))
    mixed = jax.random.permutation(jax.random.fold_in(own, 3), count)
    source_of, receiver = mixed[0:count // 2 * 2:2], mixed[1:count // 2 * 2:2]
    room = jnp.minimum(sizes[source_of] - 1, reach - sizes[receiver]) // 2
    room = jnp.where((source_of == ranking[0]) | (receiver == ranking[0]) | (sizes[receiver] == 0), 0, jnp.maximum(room, 0))
    shifted = jax.random.randint(jax.random.fold_in(own, 4), (count // 2,), 0, 1 << 20) % (room + 1)
    sizes = sizes.at[source_of].add(-shifted).at[receiver].add(shifted)
    labels = jnp.searchsorted(jnp.cumsum(sizes), jnp.arange(rows * top), side="right").astype(jnp.int32)
    table = labels.reshape(top, rows).T
    table = table[jax.random.permutation(jax.random.fold_in(own, 1), rows)]
    turn = jax.random.randint(jax.random.fold_in(own, 2), (rows, 1), 0, top)
    return jnp.take_along_axis(table, (jnp.arange(top)[None, :] + turn) % top, axis=1)


def load_shares(amount, total, limit, lean, full):
    loads = [(1 << 20) // math.isqrt(standing ** lean) + 1 for standing in range(1, amount + 1)]
    largest = limit if full else min(limit, max(-(-total // amount), total * loads[0] // sum(loads)))
    least = 1 if total - largest >= amount - 1 else 0
    holding, surplus = [largest] + [least] * (amount - 1), total - largest - least * (amount - 1)
    while surplus > 0:
        candidates = [i for i in range(1, amount) if holding[i] < largest] or [i for i in range(1, amount) if holding[i] < limit]
        mass, left = sum([loads[i] for i in candidates]), surplus
        for i in candidates:
            addition = min(limit - holding[i], max(1, left * loads[i] // mass), surplus)
            holding[i] = holding[i] + addition
            surplus = surplus - addition
    return np.array(holding)


def bell_draw(own_key, extent, width, limit, cuts=(), kind=jnp.bfloat16):
    array = width * jax.random.normal(own_key, extent, jnp.float32)
    if cuts:
        array = array * level_of(own_key, extent, cuts, -0.22, 0.18)
    return jnp.clip(array, -limit, limit).astype(kind)


def setup_inputs(seed: int = 0) -> dict:
    splits = jax.random.split(jax.random.key(seed), 8)
    grads = bell_draw(splits[0], (TOTAL_ROWS, D), 1.0, 6.0, ((0, 512),), jnp.float32)
    owners_keys = jax.random.split(jax.random.fold_in(splits[1], 1), TOTAL_ROWS // G_DEV)
    owners_turns = jax.random.permutation(jax.random.fold_in(splits[1], 3), TOTAL_ROWS // G_DEV)
    owners = jax.vmap(lambda own, number: shared_out(jax.random.fold_in(splits[1], 2), own, number, G_DEV, N_ROWS, 1, CAP, 2))(owners_keys, owners_turns).reshape((TOTAL_ROWS, 1))
    local_ids = with_ends(skewed_ids(splits[2], (TOTAL_ROWS,), OWN, 2), jax.random.fold_in(splits[2], 3), 0, OWN - 1).astype(jnp.int32)
    params = bell_draw(splits[3], (ITEMS, D), 1.0, 6.0, ((0, 64), (1, 8)), jnp.float32)
    first_moment = bell_draw(splits[4], (ITEMS, D), 0.3, 4.0, ((0, 64), (1, 8)), jnp.float32)
    second_moment = jnp.clip(jnp.exp(math.log(0.01) - 4.6051702 * jax.random.uniform(splits[5], (ITEMS, D), jnp.float32) ** level_of(splits[5], (ITEMS, D), ((0, 64), (1, 8)), -0.2, 0.2)), 0.0001, 0.01)
    step_count = jax.random.randint(splits[6], (1,), 1, 30).astype(jnp.int32)
    return dict(grads=grads, owners=owners, local_ids=local_ids, params=params, first_moment=first_moment, second_moment=second_moment, step_count=step_count)


def reference(grads, owners, local_ids, params, first_moment, second_moment, step_count):
    item = (owners[:, 0] * OWN + local_ids).astype(jnp.int32)
    summed = jnp.zeros((ITEMS, D), jnp.float32).at[item].add(grads)
    touched = jnp.zeros((ITEMS,), jnp.float32).at[item].add(1.0)
    live = (touched > 0.0)[:, None]
    new_first = jnp.where(live, 0.9 * first_moment + 0.1 * summed, first_moment)
    new_second = jnp.where(live, 0.999 * second_moment + 0.001 * summed * summed, second_moment)
    steps_done = step_count[0].astype(jnp.float32)
    fix_first = 1.0 - jnp.power(jnp.float32(0.9), steps_done)
    fix_second = 1.0 - jnp.power(jnp.float32(0.999), steps_done)
    direction = -(new_first / fix_first) / (jnp.sqrt(new_second / fix_second) + 1e-08)
    new_params = jnp.where(live, params + 0.01 * direction, params)
    row_steps = direction.astype(jnp.bfloat16)[item]
    return (new_params, new_first, new_second, row_steps)
```

```python
import functools

import jax
import jax.numpy as jnp
from jax import lax
from jax.experimental import pallas as pl
from jax.experimental.pallas import tpu as pltpu
from jax.sharding import PartitionSpec as P

LANES = 128
FULL = 32767.0
BIAS = 128.0
ORDER = ("cols", "rows")


def iota(shape, axis):
    return lax.broadcasted_iota(jnp.int32, shape, axis)


def dot(a, b):
    return jnp.dot(a, b, preferred_element_type=jnp.float32)


def dot_t(a, b):
    return lax.dot_general(a, b, (((0,), (0,)), ((), ())), preferred_element_type=jnp.float32)


def pack_kernel(groups, cap, owners_ref, ids_ref, grads_ref, message_ref, select_ref):
    count, width = grads_ref.shape
    words = cap // 2
    block = words + 1
    owner = owners_ref[...]
    mine = (owner == iota((count, LANES), 1)).astype(jnp.bfloat16)
    square = (count, count)
    earlier = (iota(square, 1) < iota(square, 0)).astype(jnp.bfloat16)
    before = dot(earlier, mine) * mine.astype(jnp.float32)
    position = jnp.sum(before, axis=1, keepdims=True).astype(jnp.int32)
    on_diagonal = iota(square, 0) == iota(square, 1)
    ids = jnp.sum(jnp.where(on_diagonal, ids_ref[...].astype(jnp.float32), 0.0), axis=1, keepdims=True)
    slots = iota((count, groups * cap), 1)
    select_ref[...] = (slots == owner * cap + position).astype(jnp.bfloat16)
    place = (slots == position * groups + owner).astype(jnp.bfloat16)

    grads = grads_ref[...]
    size = jnp.abs(grads)
    top = jnp.max(size, axis=1, keepdims=True)
    power = jnp.clip(jnp.ceil(jnp.log2(top)), -120.0, 100.0)
    code = jnp.minimum(jnp.floor(jnp.sqrt(size * jnp.exp2(-power)) * FULL + 0.5), FULL)
    code = jnp.where(grads < 0.0, -code, code)
    high = jnp.floor(code * (1.0 / 256.0) + 0.5)
    low = code - high * 256.0
    placed = dot_t(place, high.astype(jnp.bfloat16)) * 256.0 + dot_t(place, low.astype(jnp.bfloat16))
    placed = placed.astype(jnp.int32)

    named = ids + 1.0
    named_high = jnp.floor(named * (1.0 / 32.0))
    named_low = named - named_high * 32.0
    lane = iota((count, LANES), 1)
    facts = jnp.where(lane == position, named_high, 0.0)
    facts = facts + jnp.where(lane == position + cap, named_low, 0.0)
    facts = facts + jnp.where(lane == position + 2 * cap, power + BIAS, 0.0)
    facts = dot_t(mine, facts.astype(jnp.bfloat16))[:groups].astype(jnp.int32)

    for j in range(words):
        one = placed[j * groups : (j + 1) * groups]
        two = placed[(j + words) * groups : (j + words + 1) * groups]
        word = (one & 0xFFFF) | (two << 16)
        for c in range(width // LANES):
            rows = pl.ds(c * groups * block + j, groups, stride=block)
            message_ref[rows, :] = word[:, c * LANES : (c + 1) * LANES]
    for c in range(width // LANES):
        message_ref[pl.ds(c * groups * block + words, groups, stride=block), :] = facts


def update_kernel(
    cap, message_ref, fix_ref, params_ref, first_ref, second_ref,
    new_params_ref, new_first_ref, new_second_ref, answer_ref, spread_ref,
):
    own, lanes = params_ref.shape
    words = cap // 2
    block = words + 1
    sources = message_ref.shape[0] // block
    facts = message_ref[pl.ds(words, sources, stride=block), :].astype(jnp.float32)
    across = facts.T
    id_rows = (across[:cap] * 32.0 + across[cap : 2 * cap] - 1.0).astype(jnp.int32)
    items = iota((own, sources), 0)
    total = jnp.zeros((own, 2 * lanes), jnp.float32)
    seen = jnp.zeros((own, sources), jnp.bfloat16)
    for j in range(words):
        word = message_ref[pl.ds(j, sources, stride=block), :]
        for s, code in ((j, (word << 16) >> 16), (j + words, word >> 16)):
            scale = jnp.exp2(facts[:, 2 * cap + s : 2 * cap + s + 1] - BIAS) * (1.0 / (FULL * FULL))
            code = code.astype(jnp.float32)
            value = code * jnp.abs(code) * scale
            high = value.astype(jnp.bfloat16)
            low = (value - high.astype(jnp.float32)).astype(jnp.bfloat16)
            hit = (items == id_rows[s : s + 1]).astype(jnp.bfloat16)
            total = total + dot(hit, jnp.concatenate([high, low], axis=1))
            seen = jnp.maximum(seen, hit)
    summed = total[:, :lanes] + total[:, lanes:]
    live = jnp.max(seen.astype(jnp.float32), axis=1, keepdims=True) > 0.0
    first, second, params = first_ref[...], second_ref[...], params_ref[...]
    new_first = jnp.where(live, 0.9 * first + 0.1 * summed, first)
    new_second = jnp.where(live, 0.999 * second + 0.001 * summed * summed, second)
    direction = -(new_first / fix_ref[0]) / (jnp.sqrt(new_second / fix_ref[1]) + 1e-08)
    new_first_ref[...] = new_first
    new_second_ref[...] = new_second
    new_params_ref[...] = jnp.where(live, params + 0.01 * direction, params)

    half = own // 2
    direction = direction.astype(jnp.bfloat16)
    table = jnp.concatenate([direction[:half], direction[half:]], axis=1)
    spots = iota((sources, half), 1)
    for s in range(cap):
        id_col = (facts[:, s : s + 1] * 32.0 + facts[:, cap + s : cap + s + 1] - 1.0).astype(jnp.int32)
        upper = id_col >= half
        hit = (spots == jnp.where(upper, id_col - half, id_col)).astype(jnp.bfloat16)
        both = dot(hit, table)
        spread_ref[pl.ds(s, sources, stride=cap), :] = jnp.where(upper, both[:, lanes:], both[:, :lanes])
    answer_ref[...] = spread_ref[...].astype(jnp.bfloat16)


def unpack_kernel(select_ref, back_ref, out_ref):
    select = select_ref[...]
    slots = select.shape[1]
    for c in range(out_ref.shape[1] // LANES):
        rows = dot(select, back_ref[c * slots : (c + 1) * slots])
        out_ref[:, c * LANES : (c + 1) * LANES] = rows.astype(jnp.bfloat16)


VMEM = pl.BlockSpec(memory_space=pltpu.VMEM)
SMEM = pl.BlockSpec(memory_space=pltpu.SMEM)


def params_for(mib):
    return pltpu.CompilerParams(vmem_limit_bytes=mib * 1024 * 1024)


def local(grads, owners, local_ids, params, first_moment, second_moment, step_count):
    groups = lax.axis_size("rows")
    slices = lax.axis_size("cols")
    count, width = grads.shape
    own, lanes = params.shape
    cap = max(2, 2 * count // groups)
    block = cap // 2 + 1
    peers = groups * slices
    message, select = pl.pallas_call(
        functools.partial(pack_kernel, groups, cap),
        out_shape=(
            jax.ShapeDtypeStruct((peers * block, lanes), jnp.int32),
            jax.ShapeDtypeStruct((count, groups * cap), jnp.bfloat16),
        ),
        in_specs=[VMEM, VMEM, VMEM],
        out_specs=(VMEM, VMEM),
        compiler_params=params_for(40),
        name="pack",
    )(owners, local_ids.reshape(1, count), grads)
    message = message.reshape(peers, 1, block * lanes)
    message = lax.all_to_all(message, ORDER, split_axis=0, concat_axis=0, tiled=True)
    message = message.reshape(peers * block, lanes)
    steps_done = step_count[0].astype(jnp.float32)
    fix_first = 1.0 - jnp.power(jnp.float32(0.9), steps_done)
    fix_second = 1.0 - jnp.power(jnp.float32(0.999), steps_done)
    table = jax.ShapeDtypeStruct((own, lanes), jnp.float32)
    new_params, new_first, new_second, answer = pl.pallas_call(
        functools.partial(update_kernel, cap),
        out_shape=(table, table, table, jax.ShapeDtypeStruct((peers * cap, lanes), jnp.bfloat16)),
        in_specs=[VMEM, SMEM, VMEM, VMEM, VMEM],
        out_specs=(VMEM, VMEM, VMEM, VMEM),
        scratch_shapes=[pltpu.VMEM((peers * cap, lanes), jnp.float32)],
        compiler_params=params_for(48),
        name="update",
    )(message, jnp.stack([fix_first, fix_second]), params, first_moment, second_moment)
    answer = answer.reshape(peers, cap, lanes)
    answer = lax.all_to_all(answer, ORDER, split_axis=0, concat_axis=0, tiled=True)
    row_steps = pl.pallas_call(
        unpack_kernel,
        out_shape=jax.ShapeDtypeStruct((count, width), jnp.bfloat16),
        in_specs=[VMEM, VMEM],
        out_specs=VMEM,
        compiler_params=params_for(40),
        name="unpack",
    )(select, answer.reshape(peers * cap, lanes))
    return (new_params, new_first, new_second, row_steps)


def solution(mesh):
    placed = (
        P(("rows", "cols"), None),
        P(("rows", "cols"), None),
        P(("rows", "cols")),
        P("rows", "cols"),
        P("rows", "cols"),
        P("rows", "cols"),
        P(),
    )
    return jax.shard_map(
        local,
        mesh=mesh,
        in_specs=placed,
        out_specs=(
            P("rows", "cols"),
            P("rows", "cols"),
            P("rows", "cols"),
            P(("rows", "cols"), None),
        ),
        check_vma=False,
    )
```

```python
import functools

import jax
import jax.numpy as jnp
from jax import lax
from jax.experimental import pallas as pl
from jax.experimental.pallas import tpu as pltpu
from jax.sharding import PartitionSpec as P

LANES = 128
FULL = 32767.0
ORDER = ("cols", "rows")


def iota(shape, axis):
    return lax.broadcasted_iota(jnp.int32, shape, axis)


def dot(a, b):
    return jnp.dot(a, b, preferred_element_type=jnp.float32)


def dot_t(a, b):
    return lax.dot_general(a, b, (((0,), (0,)), ((), ())), preferred_element_type=jnp.float32)


def pack_kernel(groups, cap, own, items_ref, grads_ref, message_ref, select_ref):
    count, width = grads_ref.shape
    words = cap // 2
    block = words + 1
    square = (count, count)
    on_diagonal = iota(square, 0) == iota(square, 1)
    item = items_ref[0:1] * own + items_ref[1:2]
    item = jnp.sum(jnp.where(on_diagonal, item.astype(jnp.float32), 0.0), axis=1, keepdims=True)
    item = item.astype(jnp.int32)
    owner = lax.div(item, own)
    mine = (owner == iota((count, LANES), 1)).astype(jnp.bfloat16)
    earlier = (iota(square, 1) < iota(square, 0)).astype(jnp.bfloat16)
    before = dot(earlier, mine) * mine.astype(jnp.float32)
    position = jnp.sum(before, axis=1, keepdims=True).astype(jnp.int32)
    slots = iota((count, groups * cap), 1)
    select_ref[...] = (slots == owner * cap + position).astype(jnp.bfloat16)
    place = (slots == position * groups + owner).astype(jnp.bfloat16)

    grads = grads_ref[...]
    size = jnp.abs(grads)
    top = jnp.max(size, axis=1, keepdims=True)
    power = jnp.clip(jnp.ceil(jnp.log2(top)), -120.0, 100.0)
    code = jnp.minimum(jnp.floor(jnp.sqrt(size * jnp.exp2(-power)) * FULL + 0.5), FULL)
    code = jnp.where(grads < 0.0, -code, code)
    high = jnp.floor(code * (1.0 / 256.0) + 0.5)
    low = code - high * 256.0

    named = lax.rem(item, own) + 1
    lane = iota((count, LANES), 1)
    at_id = lane == position
    at_power = lane == position + cap
    facts_high = jnp.where(at_id, lax.div(named, 32).astype(jnp.float32), 0.0)
    facts_low = jnp.where(at_id, lax.rem(named, 32).astype(jnp.float32), jnp.where(at_power, power, 0.0))
    facts = dot_t(mine, facts_high.astype(jnp.bfloat16)) * 32.0 + dot_t(mine, facts_low.astype(jnp.bfloat16))
    facts = facts[:groups].astype(jnp.int32)

    placed = dot_t(place, high.astype(jnp.bfloat16)) * 256.0 + dot_t(place, low.astype(jnp.bfloat16))
    placed = placed.astype(jnp.int32)
    for j in range(words):
        one = placed[j * groups : (j + 1) * groups]
        two = placed[(j + words) * groups : (j + words + 1) * groups]
        word = (one & 0xFFFF) | (two << 16)
        for c in range(width // LANES):
            rows = pl.ds(c * groups * block + j, groups, stride=block)
            message_ref[rows, :] = word[:, c * LANES : (c + 1) * LANES]
    for c in range(width // LANES):
        message_ref[pl.ds(c * groups * block + words, groups, stride=block), :] = facts


def update_kernel(
    cap, message_ref, fix_ref, params_ref, first_ref, second_ref,
    new_params_hbm, new_first_hbm, new_second_hbm, answer_ref, spread_ref, table_ref, table_sem,
):
    own, lanes = params_ref.shape
    words = cap // 2
    block = words + 1
    sources = message_ref.shape[0] // block
    facts = message_ref[pl.ds(words, sources, stride=block), :]
    across = facts.astype(jnp.float32).T
    id_rows = across[:cap].astype(jnp.int32) - 1
    scale_rows = jnp.exp2(across[cap : 2 * cap]).astype(jnp.bfloat16)
    short_rows = id_rows.astype(jnp.int16)
    items = iota((own, sources), 0).astype(jnp.int16)
    total = jnp.zeros((own, 2 * lanes), jnp.float32)
    for j in range(words):
        word = message_ref[pl.ds(j, sources, stride=block), :]
        for s, code in ((j, (word << 16) >> 16), (j + words, word >> 16)):
            code = code.astype(jnp.float32)
            value = code * jnp.abs(code)
            high = value.astype(jnp.bfloat16)
            low = (value - high.astype(jnp.float32)).astype(jnp.bfloat16)
            hit = jnp.where(items == short_rows[s : s + 1], scale_rows[s : s + 1], jnp.bfloat16(0))
            total = total + dot(hit, jnp.concatenate([high, low], axis=1))
    fine = 32
    coarse = own // fine
    counts = jnp.zeros((coarse, fine), jnp.float32)
    for s in range(cap):
        row = id_rows[s : s + 1]
        whole = (iota((coarse, sources), 0) == lax.div(row, fine)).astype(jnp.bfloat16)
        rest = (iota((fine, sources), 0) == lax.rem(row, fine)).astype(jnp.bfloat16)
        counts = counts + lax.dot_general(whole, rest, (((1,), (1,)), ((), ())), preferred_element_type=jnp.float32)
    counts = jnp.minimum(counts, 1.0).astype(jnp.bfloat16)
    whole = (lax.div(iota((own, coarse), 0), fine) == iota((own, coarse), 1)).astype(jnp.bfloat16)
    rest = lax.rem(iota((own, fine), 0), fine) == iota((own, fine), 1)
    live = jnp.sum(jnp.where(rest, dot(whole, counts), 0.0), axis=1, keepdims=True) > 0.0
    summed = (total[:, :lanes] + total[:, lanes:]) * (1.0 / (FULL * FULL))
    first, second, params = first_ref[...], second_ref[...], params_ref[...]
    new_first = jnp.where(live, 0.9 * first + 0.1 * summed, first)
    new_second = jnp.where(live, 0.999 * second + 0.001 * summed * summed, second)
    direction = -(new_first / fix_ref[0]) / (jnp.sqrt(new_second / fix_ref[1]) + 1e-08)
    table_ref[0] = jnp.where(live, params + 0.01 * direction, params)
    table_ref[1] = new_first
    table_ref[2] = new_second
    copies = [
        pltpu.make_async_copy(table_ref.at[n], out, table_sem.at[n])
        for n, out in enumerate((new_params_hbm, new_first_hbm, new_second_hbm))
    ]
    for copy in copies:
        copy.start()

    half = own // 2
    direction = direction.astype(jnp.bfloat16)
    table = jnp.concatenate([direction[:half], direction[half:]], axis=1)
    spots = iota((sources, half), 1).astype(jnp.int16)
    ids = facts - 1
    for s in range(cap):
        wanted = jnp.broadcast_to(ids[:, s : s + 1], (sources, lanes))
        upper = wanted >= half
        spot = jnp.where(upper, wanted - half, wanted).astype(jnp.int16)
        hit = (spots == jnp.concatenate([spot] * (half // lanes), axis=1)).astype(jnp.bfloat16)
        both = dot(hit, table)
        spread_ref[pl.ds(s, sources, stride=cap), :] = jnp.where(upper, both[:, lanes:], both[:, :lanes])
    answer_ref[...] = spread_ref[...].astype(jnp.bfloat16)
    for copy in copies:
        copy.wait()


def unpack_kernel(select_ref, back_ref, out_ref):
    select = select_ref[...]
    slots = select.shape[1]
    for c in range(out_ref.shape[1] // LANES):
        rows = dot(select, back_ref[c * slots : (c + 1) * slots])
        out_ref[:, c * LANES : (c + 1) * LANES] = rows.astype(jnp.bfloat16)


VMEM = pl.BlockSpec(memory_space=pltpu.VMEM)
HBM = pl.BlockSpec(memory_space=pltpu.HBM)
SMEM = pl.BlockSpec(memory_space=pltpu.SMEM)


def params_for(mib):
    return pltpu.CompilerParams(vmem_limit_bytes=mib * 1024 * 1024)


def local(grads, owners, local_ids, params, first_moment, second_moment, step_count):
    groups = lax.axis_size("rows")
    slices = lax.axis_size("cols")
    count, width = grads.shape
    own, lanes = params.shape
    cap = max(2, 2 * count // groups)
    block = cap // 2 + 1
    peers = groups * slices
    items = jnp.concatenate([owners.reshape(1, count), local_ids.reshape(1, count)], axis=0)
    message, select = pl.pallas_call(
        functools.partial(pack_kernel, groups, cap, own),
        out_shape=(
            jax.ShapeDtypeStruct((peers * block, lanes), jnp.int32),
            jax.ShapeDtypeStruct((count, groups * cap), jnp.bfloat16),
        ),
        in_specs=[VMEM, VMEM],
        out_specs=(VMEM, VMEM),
        compiler_params=params_for(40),
        name="pack",
    )(items, grads)
    message = message.reshape(peers, 1, block * lanes)
    message = lax.all_to_all(message, ORDER, split_axis=0, concat_axis=0, tiled=True)
    message = message.reshape(peers * block, lanes)
    steps_done = step_count[0].astype(jnp.float32)
    fix_first = 1.0 - jnp.power(jnp.float32(0.9), steps_done)
    fix_second = 1.0 - jnp.power(jnp.float32(0.999), steps_done)
    table = jax.ShapeDtypeStruct((own, lanes), jnp.float32)
    new_params, new_first, new_second, answer = pl.pallas_call(
        functools.partial(update_kernel, cap),
        out_shape=(table, table, table, jax.ShapeDtypeStruct((peers * cap, lanes), jnp.bfloat16)),
        in_specs=[VMEM, SMEM, VMEM, VMEM, VMEM],
        out_specs=(HBM, HBM, HBM, VMEM),
        scratch_shapes=[
            pltpu.VMEM((peers * cap, lanes), jnp.float32),
            pltpu.VMEM((3, own, lanes), jnp.float32),
            pltpu.SemaphoreType.DMA((3,)),
        ],
        compiler_params=params_for(48),
        name="update",
    )(message, jnp.stack([fix_first, fix_second]), params, first_moment, second_moment)
    answer = answer.reshape(peers, cap, lanes)
    answer = lax.all_to_all(answer, ORDER, split_axis=0, concat_axis=0, tiled=True)
    row_steps = pl.pallas_call(
        unpack_kernel,
        out_shape=jax.ShapeDtypeStruct((count, width), jnp.bfloat16),
        in_specs=[VMEM, VMEM],
        out_specs=VMEM,
        compiler_params=params_for(40),
        name="unpack",
    )(select, answer.reshape(peers * cap, lanes))
    return (new_params, new_first, new_second, row_steps)


def solution(mesh):
    placed = (
        P(("rows", "cols"), None),
        P(("rows", "cols"), None),
        P(("rows", "cols")),
        P("rows", "cols"),
        P("rows", "cols"),
        P("rows", "cols"),
        P(),
    )
    return jax.shard_map(
        local,
        mesh=mesh,
        in_specs=placed,
        out_specs=(
            P("rows", "cols"),
            P("rows", "cols"),
            P("rows", "cols"),
            P(("rows", "cols"), None),
        ),
        check_vma=False,
    )
```

```python
import functools

import jax
import jax.numpy as jnp
from jax import lax
from jax.experimental import pallas as pl
from jax.experimental.pallas import tpu as pltpu
from jax.sharding import PartitionSpec as P

LANES = 128
FULL = 32767.0
ORDER = ("cols", "rows")


def iota(shape, axis):
    return lax.broadcasted_iota(jnp.int32, shape, axis)


def dot(a, b):
    return jnp.dot(a, b, preferred_element_type=jnp.float32)


def dot_nt(a, b):
    return lax.dot_general(a, b, (((1,), (1,)), ((), ())), preferred_element_type=jnp.float32)


def pack_kernel(groups, cap, own, names_ref, grads_ref, message_ref, select_ref):
    count, width = grads_ref.shape
    words = cap // 2
    block = words + 1
    slices = width // LANES
    share = groups * block
    owner = names_ref[0:1]
    mine = owner == iota((groups, count), 0)
    mine_half = mine.astype(jnp.bfloat16)
    square = (count, count)
    earlier = (iota(square, 0) < iota(square, 1)).astype(jnp.bfloat16)
    before = jnp.where(mine, dot(mine_half, earlier), 0.0)
    position = jnp.sum(before, axis=0, keepdims=True).astype(jnp.int32)
    place = (iota((groups * cap, count), 0) == position * groups + owner).astype(jnp.bfloat16)
    on_diagonal = iota(square, 0) == iota(square, 1)

    grads = grads_ref[...]
    size = jnp.abs(grads)
    top = jnp.max(size, axis=1, keepdims=True)
    power = jnp.clip(jnp.ceil(jnp.log2(top)), -120.0, 100.0)
    code = jnp.minimum(jnp.floor(jnp.sqrt(size * jnp.exp2(-power)) * FULL + 0.5), FULL)
    code = jnp.where(grads < 0.0, -code, code)
    high = jnp.floor(code * (1.0 / 256.0) + 0.5)
    low = (code - high * 256.0).astype(jnp.bfloat16)
    high = high.astype(jnp.bfloat16)

    power_row = jnp.sum(jnp.where(on_diagonal, power, 0.0), axis=0, keepdims=True)
    named = names_ref[1:2] + 1
    lane = iota((LANES, count), 0)
    at_id = lane == position
    at_power = lane == position + cap
    facts_high = jnp.where(at_id, lax.div(named, 32).astype(jnp.float32), 0.0).astype(jnp.bfloat16)
    facts_low = jnp.where(at_id, lax.rem(named, 32).astype(jnp.float32), jnp.where(at_power, power_row, 0.0))
    facts = dot_nt(mine_half, facts_high) * 32.0 + dot_nt(mine_half, facts_low.astype(jnp.bfloat16))
    facts = facts.astype(jnp.int32)

    for c in range(slices):
        columns = slice(c * LANES, (c + 1) * LANES)
        placed = dot(place, jnp.concatenate([high[:, columns], low[:, columns]], axis=1))
        placed = (placed[:, :LANES] * 256.0 + placed[:, LANES:]).astype(jnp.int32)
        for j in range(words):
            one = placed[j * groups : (j + 1) * groups]
            two = placed[(j + words) * groups : (j + words + 1) * groups]
            message_ref[pl.ds(c * share + j, groups, stride=block), :] = (one & 0xFFFF) | (two << 16)
        message_ref[pl.ds(c * share + words, groups, stride=block), :] = facts

    target = (owner * cap + position).astype(jnp.float32)
    target = jnp.sum(jnp.where(on_diagonal, target, 0.0), axis=1, keepdims=True).astype(jnp.int32)
    select_ref[...] = (iota((count, groups * cap), 1) == target).astype(jnp.bfloat16)


def update_kernel(
    cap, message_ref, fix_ref, params_ref, first_ref, second_ref,
    new_params_hbm, new_first_hbm, new_second_hbm, answer_ref, spread_ref, table_ref, table_sem,
):
    own, lanes = params_ref.shape
    words = cap // 2
    block = words + 1
    sources = message_ref.shape[0] // block
    facts = message_ref[pl.ds(words, sources, stride=block), :]
    across = facts.astype(jnp.float32).T
    id_rows = across[:cap].astype(jnp.int32) - 1
    scale_rows = jnp.exp2(across[cap : 2 * cap]).astype(jnp.bfloat16)
    short_rows = id_rows.astype(jnp.int16)
    items = iota((own, sources), 0).astype(jnp.int16)
    total = jnp.zeros((own, 2 * lanes), jnp.float32)
    for j in range(words):
        word = message_ref[pl.ds(j, sources, stride=block), :]
        for s, code in ((j, (word << 16) >> 16), (j + words, word >> 16)):
            code = code.astype(jnp.float32)
            value = code * jnp.abs(code)
            high = value.astype(jnp.bfloat16)
            low = (value - high.astype(jnp.float32)).astype(jnp.bfloat16)
            hit = jnp.where(items == short_rows[s : s + 1], scale_rows[s : s + 1], jnp.bfloat16(0))
            total = total + dot(hit, jnp.concatenate([high, low], axis=1))
    fine = 32
    coarse = own // fine
    counts = jnp.zeros((coarse, fine), jnp.float32)
    for s in range(cap):
        row = id_rows[s : s + 1]
        whole = (iota((coarse, sources), 0) == lax.div(row, fine)).astype(jnp.bfloat16)
        rest = (iota((fine, sources), 0) == lax.rem(row, fine)).astype(jnp.bfloat16)
        counts = counts + dot_nt(whole, rest)
    counts = jnp.minimum(counts, 1.0).astype(jnp.bfloat16)
    whole = (lax.div(iota((own, coarse), 0), fine) == iota((own, coarse), 1)).astype(jnp.bfloat16)
    rest = lax.rem(iota((own, fine), 0), fine) == iota((own, fine), 1)
    live = jnp.sum(jnp.where(rest, dot(whole, counts), 0.0), axis=1, keepdims=True) > 0.0
    summed = (total[:, :lanes] + total[:, lanes:]) * (1.0 / (FULL * FULL))
    first, second, params = first_ref[...], second_ref[...], params_ref[...]
    new_first = jnp.where(live, 0.9 * first + 0.1 * summed, first)
    new_second = jnp.where(live, 0.999 * second + 0.001 * summed * summed, second)
    direction = -(new_first / fix_ref[0]) / (jnp.sqrt(new_second / fix_ref[1]) + 1e-08)
    table_ref[0] = jnp.where(live, params + 0.01 * direction, params)
    table_ref[1] = new_first
    table_ref[2] = new_second
    copies = [
        pltpu.make_async_copy(table_ref.at[n], out, table_sem.at[n])
        for n, out in enumerate((new_params_hbm, new_first_hbm, new_second_hbm))
    ]
    for copy in copies:
        copy.start()

    half = own // 2
    direction = direction.astype(jnp.bfloat16)
    table = jnp.concatenate([direction[:half], direction[half:]], axis=1)
    spots = iota((sources, half), 1).astype(jnp.int16)
    ids = facts - 1
    for s in range(cap):
        wanted = jnp.broadcast_to(ids[:, s : s + 1], (sources, lanes))
        upper = wanted >= half
        spot = jnp.where(upper, wanted - half, wanted).astype(jnp.int16)
        hit = (spots == jnp.concatenate([spot] * (half // lanes), axis=1)).astype(jnp.bfloat16)
        both = dot(hit, table)
        spread_ref[pl.ds(s, sources, stride=cap), :] = jnp.where(upper, both[:, lanes:], both[:, :lanes])
    answer_ref[...] = spread_ref[...].astype(jnp.bfloat16)
    for copy in copies:
        copy.wait()


def unpack_kernel(select_ref, back_ref, out_ref):
    select = select_ref[...]
    slots = select.shape[1]
    for c in range(out_ref.shape[1] // LANES):
        rows = dot(select, back_ref[c * slots : (c + 1) * slots])
        out_ref[:, c * LANES : (c + 1) * LANES] = rows.astype(jnp.bfloat16)


VMEM = pl.BlockSpec(memory_space=pltpu.VMEM)
HBM = pl.BlockSpec(memory_space=pltpu.HBM)
SMEM = pl.BlockSpec(memory_space=pltpu.SMEM)


def params_for(mib):
    return pltpu.CompilerParams(vmem_limit_bytes=mib * 1024 * 1024)


def local(grads, owners, local_ids, params, first_moment, second_moment, step_count):
    groups = lax.axis_size("rows")
    slices = lax.axis_size("cols")
    count, width = grads.shape
    own, lanes = params.shape
    cap = max(2, 2 * count // groups)
    block = cap // 2 + 1
    peers = groups * slices
    steps_done = step_count[0].astype(jnp.float32)
    fix_first = 1.0 - jnp.power(jnp.float32(0.9), steps_done)
    fix_second = 1.0 - jnp.power(jnp.float32(0.999), steps_done)
    fixes = jnp.stack([fix_first, fix_second])
    names = jnp.concatenate([owners.reshape(1, count), local_ids.reshape(1, count)], axis=0)
    names, fixes = lax.optimization_barrier((names, fixes))
    message, select = pl.pallas_call(
        functools.partial(pack_kernel, groups, cap, own),
        out_shape=(
            jax.ShapeDtypeStruct((peers * block, lanes), jnp.int32),
            jax.ShapeDtypeStruct((count, groups * cap), jnp.bfloat16),
        ),
        in_specs=[VMEM, VMEM],
        out_specs=(VMEM, VMEM),
        compiler_params=params_for(40),
        name="pack",
    )(names, grads)
    message = message.reshape(peers, 1, block * lanes)
    message = lax.all_to_all(message, ORDER, split_axis=0, concat_axis=0, tiled=True)
    message = message.reshape(peers * block, lanes)
    table = jax.ShapeDtypeStruct((own, lanes), jnp.float32)
    new_params, new_first, new_second, answer = pl.pallas_call(
        functools.partial(update_kernel, cap),
        out_shape=(table, table, table, jax.ShapeDtypeStruct((peers * cap, lanes), jnp.bfloat16)),
        in_specs=[VMEM, SMEM, VMEM, VMEM, VMEM],
        out_specs=(HBM, HBM, HBM, VMEM),
        scratch_shapes=[
            pltpu.VMEM((peers * cap, lanes), jnp.float32),
            pltpu.VMEM((3, own, lanes), jnp.float32),
            pltpu.SemaphoreType.DMA((3,)),
        ],
        compiler_params=params_for(48),
        name="update",
    )(message, fixes, params, first_moment, second_moment)
    answer = answer.reshape(peers, cap, lanes)
    answer = lax.all_to_all(answer, ORDER, split_axis=0, concat_axis=0, tiled=True)
    row_steps = pl.pallas_call(
        unpack_kernel,
        out_shape=jax.ShapeDtypeStruct((count, width), jnp.bfloat16),
        in_specs=[VMEM, VMEM],
        out_specs=VMEM,
        compiler_params=params_for(40),
        name="unpack",
    )(select, answer.reshape(peers * cap, lanes))
    return (new_params, new_first, new_second, row_steps)


def solution(mesh):
    placed = (
        P(("rows", "cols"), None),
        P(("rows", "cols"), None),
        P(("rows", "cols")),
        P("rows", "cols"),
        P("rows", "cols"),
        P("rows", "cols"),
        P(),
    )
    return jax.shard_map(
        local,
        mesh=mesh,
        in_specs=placed,
        out_specs=(
            P("rows", "cols"),
            P("rows", "cols"),
            P("rows", "cols"),
            P(("rows", "cols"), None),
        ),
        check_vma=False,
    )
```

```python
import functools

import jax
import jax.numpy as jnp
import numpy as np
from jax import lax
from jax.experimental import pallas as pl
from jax.experimental.pallas import tpu as pltpu
from jax.sharding import PartitionSpec as P

LANES = 128
FULL = 32767.0
ORDER = ("cols", "rows")


def iota(shape, axis):
    return lax.broadcasted_iota(jnp.int32, shape, axis)


def dot(a, b):
    return jnp.dot(a, b, preferred_element_type=jnp.float32)


def dot_nt(a, b):
    return lax.dot_general(a, b, (((1,), (1,)), ((), ())), preferred_element_type=jnp.float32)


def one_minus_power(base, steps):
    factor = 1.0 - float(np.float32(base))
    total = jnp.float32(0.0)
    for bit in range(5):
        has = ((steps >> bit) & 1).astype(jnp.float32)
        total = total + has * np.float32(factor) * (1.0 - total)
        factor = factor * (2.0 - factor)
    return total


def pack_kernel(groups, cap, own, names_ref, grads_ref, message_ref, select_ref):
    count, width = grads_ref.shape
    words = cap // 2
    block = words + 1
    slices = width // LANES
    share = groups * block
    owner = names_ref[0:1]
    mine = owner == iota((groups, count), 0)
    mine_half = mine.astype(jnp.bfloat16)
    square = (count, count)
    earlier = (iota(square, 0) < iota(square, 1)).astype(jnp.bfloat16)
    before = jnp.where(mine, dot(mine_half, earlier), 0.0)
    position = jnp.sum(before, axis=0, keepdims=True).astype(jnp.int32)
    place = (iota((groups * cap, count), 0) == position * groups + owner).astype(jnp.bfloat16)
    on_diagonal = iota(square, 0) == iota(square, 1)

    grads = grads_ref[...]
    size = jnp.abs(grads)
    top = jnp.max(size, axis=1, keepdims=True)
    power = jnp.clip(jnp.ceil(jnp.log2(top)), -120.0, 100.0)
    code = jnp.minimum(jnp.floor(jnp.sqrt(size * jnp.exp2(-power)) * FULL + 0.5), FULL)
    code = jnp.where(grads < 0.0, -code, code)
    high = jnp.floor(code * (1.0 / 256.0) + 0.5)
    low = (code - high * 256.0).astype(jnp.bfloat16)
    high = high.astype(jnp.bfloat16)

    power_row = jnp.sum(jnp.where(on_diagonal, power, 0.0), axis=0, keepdims=True)
    named = names_ref[1:2] + 1
    lane = iota((LANES, count), 0)
    at_id = lane == position
    at_power = lane == position + cap
    facts_high = jnp.where(at_id, lax.div(named, 32).astype(jnp.float32), 0.0).astype(jnp.bfloat16)
    facts_low = jnp.where(at_id, lax.rem(named, 32).astype(jnp.float32), jnp.where(at_power, power_row, 0.0))
    facts = dot_nt(mine_half, facts_high) * 32.0 + dot_nt(mine_half, facts_low.astype(jnp.bfloat16))
    facts = facts.astype(jnp.int32)

    for c in range(slices):
        columns = slice(c * LANES, (c + 1) * LANES)
        placed = dot(place, jnp.concatenate([high[:, columns], low[:, columns]], axis=1))
        placed = (placed[:, :LANES] * 256.0 + placed[:, LANES:]).astype(jnp.int32)
        for j in range(words):
            one = placed[j * groups : (j + 1) * groups]
            two = placed[(j + words) * groups : (j + words + 1) * groups]
            message_ref[pl.ds(c * share + j, groups, stride=block), :] = (one & 0xFFFF) | (two << 16)
        message_ref[pl.ds(c * share + words, groups, stride=block), :] = facts

    target = (owner * cap + position).astype(jnp.float32)
    target = jnp.sum(jnp.where(on_diagonal, target, 0.0), axis=1, keepdims=True).astype(jnp.int32)
    select_ref[...] = (iota((count, groups * cap), 1) == target).astype(jnp.bfloat16)


def update_kernel(
    cap, message_ref, step_ref, params_ref, first_ref, second_ref,
    new_params_hbm, new_first_hbm, new_second_hbm, answer_ref, spread_ref, halves_ref, table_ref, table_sem,
):
    own, lanes = params_ref.shape
    words = cap // 2
    block = words + 1
    sources = message_ref.shape[0] // block
    facts = message_ref[pl.ds(words, sources, stride=block), :]
    across = facts.astype(jnp.float32).T
    id_rows = across[:cap].astype(jnp.int32) - 1
    scale_rows = jnp.exp2(across[cap : 2 * cap]).astype(jnp.bfloat16)
    short_rows = id_rows.astype(jnp.int16)
    items = iota((own, sources), 0).astype(jnp.int16)
    total = jnp.zeros((own, 2 * lanes), jnp.float32)
    for j in range(words):
        word = message_ref[pl.ds(j, sources, stride=block), :]
        for s, code in ((j, (word << 16) >> 16), (j + words, word >> 16)):
            code = code.astype(jnp.float32)
            value = code * jnp.abs(code)
            high = value.astype(jnp.bfloat16)
            low = (value - high.astype(jnp.float32)).astype(jnp.bfloat16)
            hit = jnp.where(items == short_rows[s : s + 1], scale_rows[s : s + 1], jnp.bfloat16(0))
            total = total + dot(hit, jnp.concatenate([high, low], axis=1))
    fine = 32
    coarse = own // fine
    counts = jnp.zeros((coarse, fine), jnp.float32)
    for s in range(cap):
        row = id_rows[s : s + 1]
        whole = (iota((coarse, sources), 0) == lax.div(row, fine)).astype(jnp.bfloat16)
        rest = (iota((fine, sources), 0) == lax.rem(row, fine)).astype(jnp.bfloat16)
        counts = counts + dot_nt(whole, rest)
    counts = jnp.minimum(counts, 1.0).astype(jnp.bfloat16)
    whole = (lax.div(iota((own, coarse), 0), fine) == iota((own, coarse), 1)).astype(jnp.bfloat16)
    rest = lax.rem(iota((own, fine), 0), fine) == iota((own, fine), 1)
    live = jnp.sum(jnp.where(rest, dot(whole, counts), 0.0), axis=1, keepdims=True) > 0.0
    summed = (total[:, :lanes] + total[:, lanes:]) * (1.0 / (FULL * FULL))
    fix_first = one_minus_power(0.9, step_ref[0])
    fix_second = one_minus_power(0.999, step_ref[0])
    first, second, params = first_ref[...], second_ref[...], params_ref[...]
    new_first = jnp.where(live, 0.9 * first + 0.1 * summed, first)
    new_second = jnp.where(live, 0.999 * second + 0.001 * summed * summed, second)
    direction = -(new_first / fix_first) / (jnp.sqrt(new_second / fix_second) + 1e-08)
    table_ref[0] = jnp.where(live, params + 0.01 * direction, params)
    table_ref[1] = new_first
    table_ref[2] = new_second
    copies = [
        pltpu.make_async_copy(table_ref.at[n], out, table_sem.at[n])
        for n, out in enumerate((new_params_hbm, new_first_hbm, new_second_hbm))
    ]
    for copy in copies:
        copy.start()

    half = own // 2
    direction = direction.astype(jnp.bfloat16)
    halves_ref[...] = jnp.concatenate([direction[:half], direction[half:]], axis=1)
    part = sources // 2
    spots = iota((cap * part, half), 1).astype(jnp.int16)

    def answer_part(p, carry):
        ids = message_ref[pl.ds(p * part * block + words, part, stride=block), :] - 1
        wanted = jnp.concatenate([jnp.broadcast_to(ids[:, s : s + 1], (part, lanes)) for s in range(cap)], axis=0)
        upper = wanted >= half
        spot = jnp.where(upper, wanted - half, wanted).astype(jnp.int16)
        hit = (spots == jnp.concatenate([spot] * (half // lanes), axis=1)).astype(jnp.bfloat16)
        both = dot(hit, halves_ref[...])
        found = jnp.where(upper, both[:, lanes:], both[:, :lanes])
        for s in range(cap):
            spread_ref[pl.ds(p * part * cap + s, part, stride=cap), :] = found[s * part : (s + 1) * part]
        rows = pl.ds(pl.multiple_of(p * part * cap, part * cap), part * cap)
        answer_ref[rows, :] = spread_ref[rows, :].astype(jnp.bfloat16)
        return carry

    lax.fori_loop(0, 2, answer_part, 0)
    for copy in copies:
        copy.wait()


def unpack_kernel(select_ref, back_ref, out_hbm, out_ref, out_sem):
    select = select_ref[...]
    slots = select.shape[1]
    copies = []
    for c in range(out_ref.shape[1] // LANES):
        columns = pl.ds(c * LANES, LANES)
        rows = dot(select, back_ref[c * slots : (c + 1) * slots])
        out_ref[:, columns] = rows.astype(jnp.bfloat16)
        copies.append(pltpu.make_async_copy(out_ref.at[:, columns], out_hbm.at[:, columns], out_sem.at[c]))
        copies[-1].start()
    for copy in copies:
        copy.wait()


VMEM = pl.BlockSpec(memory_space=pltpu.VMEM)
HBM = pl.BlockSpec(memory_space=pltpu.HBM)
SMEM = pl.BlockSpec(memory_space=pltpu.SMEM)


def params_for(mib):
    return pltpu.CompilerParams(vmem_limit_bytes=mib * 1024 * 1024)


def local(grads, owners, local_ids, params, first_moment, second_moment, step_count):
    groups = lax.axis_size("rows")
    slices = lax.axis_size("cols")
    count, width = grads.shape
    own, lanes = params.shape
    cap = max(2, 2 * count // groups)
    block = cap // 2 + 1
    peers = groups * slices
    names = jnp.concatenate([owners.reshape(1, count), local_ids.reshape(1, count)], axis=0)
    message, select = pl.pallas_call(
        functools.partial(pack_kernel, groups, cap, own),
        out_shape=(
            jax.ShapeDtypeStruct((peers * block, lanes), jnp.int32),
            jax.ShapeDtypeStruct((count, groups * cap), jnp.bfloat16),
        ),
        in_specs=[VMEM, VMEM],
        out_specs=(VMEM, VMEM),
        compiler_params=params_for(40),
        name="pack",
    )(names, grads)
    message = message.reshape(peers, 1, block * lanes)
    message = lax.all_to_all(message, ORDER, split_axis=0, concat_axis=0, tiled=True)
    message = message.reshape(peers * block, lanes)
    table = jax.ShapeDtypeStruct((own, lanes), jnp.float32)
    new_params, new_first, new_second, answer = pl.pallas_call(
        functools.partial(update_kernel, cap),
        out_shape=(table, table, table, jax.ShapeDtypeStruct((peers * cap, lanes), jnp.bfloat16)),
        in_specs=[VMEM, SMEM, VMEM, VMEM, VMEM],
        out_specs=(HBM, HBM, HBM, VMEM),
        scratch_shapes=[
            pltpu.VMEM((peers * cap, lanes), jnp.float32),
            pltpu.VMEM((own // 2, 2 * lanes), jnp.bfloat16),
            pltpu.VMEM((3, own, lanes), jnp.float32),
            pltpu.SemaphoreType.DMA((3,)),
        ],
        compiler_params=params_for(48),
        name="update",
    )(message, step_count, params, first_moment, second_moment)
    answer = answer.reshape(peers, cap, lanes)
    answer = lax.all_to_all(answer, ORDER, split_axis=0, concat_axis=0, tiled=True)
    row_steps = pl.pallas_call(
        unpack_kernel,
        out_shape=jax.ShapeDtypeStruct((count, width), jnp.bfloat16),
        in_specs=[VMEM, VMEM],
        out_specs=HBM,
        scratch_shapes=[pltpu.VMEM((count, width), jnp.bfloat16), pltpu.SemaphoreType.DMA((slices,))],
        compiler_params=params_for(40),
        name="unpack",
    )(select, answer.reshape(peers * cap, lanes))
    return (new_params, new_first, new_second, row_steps)


def solution(mesh):
    placed = (
        P(("rows", "cols"), None),
        P(("rows", "cols"), None),
        P(("rows", "cols")),
        P("rows", "cols"),
        P("rows", "cols"),
        P("rows", "cols"),
        P(),
    )
    return jax.shard_map(
        local,
        mesh=mesh,
        in_specs=placed,
        out_specs=(
            P("rows", "cols"),
            P("rows", "cols"),
            P("rows", "cols"),
            P(("rows", "cols"), None),
        ),
        check_vma=False,
    )
```

```python
import functools

import jax
import jax.numpy as jnp
import numpy as np
from jax import lax
from jax.experimental import pallas as pl
from jax.experimental.pallas import tpu as pltpu
from jax.sharding import PartitionSpec as P

LANES = 128
FULL = 32767.0
ORDER = ("cols", "rows")


def iota(shape, axis):
    return lax.broadcasted_iota(jnp.int32, shape, axis)


def dot(a, b):
    return jnp.dot(a, b, preferred_element_type=jnp.float32)


def dot_nt(a, b):
    return lax.dot_general(a, b, (((1,), (1,)), ((), ())), preferred_element_type=jnp.float32)


def one_minus_power(base, steps):
    factor = 1.0 - float(np.float32(base))
    total = jnp.zeros_like(steps, jnp.float32)
    for bit in range(5):
        has = ((steps >> bit) & 1).astype(jnp.float32)
        total = total + has * np.float32(factor) * (1.0 - total)
        factor = factor * (2.0 - factor)
    return total


def pack_kernel(groups, cap, own, names_ref, grads_ref, message_ref, select_ref):
    count, width = grads_ref.shape
    words = cap // 2
    block = words + 1
    slices = width // LANES
    share = groups * block
    owner = names_ref[0:1]
    mine = owner == iota((groups, count), 0)
    mine_half = mine.astype(jnp.bfloat16)
    square = (count, count)
    earlier = (iota(square, 0) < iota(square, 1)).astype(jnp.bfloat16)
    before = jnp.where(mine, dot(mine_half, earlier), 0.0)
    position = jnp.sum(before, axis=0, keepdims=True).astype(jnp.int32)
    place = (iota((groups * cap, count), 0) == position * groups + owner).astype(jnp.bfloat16)
    on_diagonal = iota(square, 0) == iota(square, 1)

    grads = grads_ref[...]
    size = jnp.abs(grads)
    top = jnp.max(size, axis=1, keepdims=True)
    power = jnp.clip(jnp.ceil(jnp.log2(top)), -120.0, 100.0)
    code = jnp.minimum(jnp.floor(jnp.sqrt(size * jnp.exp2(-power)) * FULL + 0.5), FULL)
    code = jnp.where(grads < 0.0, -code, code)
    high = jnp.floor(code * (1.0 / 256.0) + 0.5)
    low = (code - high * 256.0).astype(jnp.bfloat16)
    high = high.astype(jnp.bfloat16)

    power_row = jnp.sum(jnp.where(on_diagonal, power, 0.0), axis=0, keepdims=True)
    named = names_ref[1:2] + 1
    lane = iota((LANES, count), 0)
    at_id = lane == position
    at_power = lane == position + cap
    facts_high = jnp.where(at_id, lax.div(named, 32).astype(jnp.float32), 0.0).astype(jnp.bfloat16)
    facts_low = jnp.where(at_id, lax.rem(named, 32).astype(jnp.float32), jnp.where(at_power, power_row, 0.0))
    facts = dot_nt(mine_half, facts_high) * 32.0 + dot_nt(mine_half, facts_low.astype(jnp.bfloat16))
    facts = facts.astype(jnp.int32)

    for c in range(slices):
        columns = slice(c * LANES, (c + 1) * LANES)
        placed = dot(place, jnp.concatenate([high[:, columns], low[:, columns]], axis=1))
        placed = (placed[:, :LANES] * 256.0 + placed[:, LANES:]).astype(jnp.int32)
        for j in range(words):
            one = placed[j * groups : (j + 1) * groups]
            two = placed[(j + words) * groups : (j + words + 1) * groups]
            message_ref[pl.ds(c * share + j, groups, stride=block), :] = (one & 0xFFFF) | (two << 16)
        message_ref[pl.ds(c * share + words, groups, stride=block), :] = facts

    target = (owner * cap + position).astype(jnp.float32)
    target = jnp.sum(jnp.where(on_diagonal, target, 0.0), axis=1, keepdims=True).astype(jnp.int32)
    select_ref[...] = (iota((count, groups * cap), 1) == target).astype(jnp.bfloat16)


def update_kernel(
    cap, message_ref, step_ref, params_ref, first_ref, second_ref,
    new_params_hbm, new_first_hbm, new_second_hbm, answer_ref, spread_ref, halves_ref, table_ref, table_sem,
):
    own, lanes = params_ref.shape
    words = cap // 2
    block = words + 1
    sources = message_ref.shape[0] // block
    facts = message_ref[pl.ds(words, sources, stride=block), :]
    across = facts.astype(jnp.float32).T
    id_rows = across[:cap].astype(jnp.int32) - 1
    scale_rows = jnp.exp2(across[cap : 2 * cap]).astype(jnp.bfloat16)
    short_rows = id_rows.astype(jnp.int16)
    items = iota((own, sources), 0).astype(jnp.int16)
    total = jnp.zeros((own, 2 * lanes), jnp.float32)
    for j in range(words):
        word = message_ref[pl.ds(j, sources, stride=block), :]
        for s, code in ((j, (word << 16) >> 16), (j + words, word >> 16)):
            code = code.astype(jnp.float32)
            value = code * jnp.abs(code)
            high = value.astype(jnp.bfloat16)
            low = (value - high.astype(jnp.float32)).astype(jnp.bfloat16)
            hit = jnp.where(items == short_rows[s : s + 1], scale_rows[s : s + 1], jnp.bfloat16(0))
            total = total + dot(hit, jnp.concatenate([high, low], axis=1))
    fine = 32
    coarse = own // fine
    counts = jnp.zeros((coarse, fine), jnp.float32)
    for s in range(cap):
        row = id_rows[s : s + 1]
        whole = (iota((coarse, sources), 0) == lax.div(row, fine)).astype(jnp.bfloat16)
        rest = (iota((fine, sources), 0) == lax.rem(row, fine)).astype(jnp.bfloat16)
        counts = counts + dot_nt(whole, rest)
    counts = jnp.minimum(counts, 1.0).astype(jnp.bfloat16)
    whole = (lax.div(iota((own, coarse), 0), fine) == iota((own, coarse), 1)).astype(jnp.bfloat16)
    rest = lax.rem(iota((own, fine), 0), fine) == iota((own, fine), 1)
    live = jnp.sum(jnp.where(rest, dot(whole, counts), 0.0), axis=1, keepdims=True) > 0.0
    summed = (total[:, :lanes] + total[:, lanes:]) * (1.0 / (FULL * FULL))
    fix_first = one_minus_power(0.9, step_ref[...])
    fix_second = one_minus_power(0.999, step_ref[...])
    first, second, params = first_ref[...], second_ref[...], params_ref[...]
    new_first = jnp.where(live, 0.9 * first + 0.1 * summed, first)
    new_second = jnp.where(live, 0.999 * second + 0.001 * summed * summed, second)
    direction = -(new_first / fix_first) / (jnp.sqrt(new_second / fix_second) + 1e-08)
    table_ref[0] = jnp.where(live, params + 0.01 * direction, params)
    table_ref[1] = new_first
    table_ref[2] = new_second
    copies = [
        pltpu.make_async_copy(table_ref.at[n], out, table_sem.at[n])
        for n, out in enumerate((new_params_hbm, new_first_hbm, new_second_hbm))
    ]
    for copy in copies:
        copy.start()

    half = own // 2
    direction = direction.astype(jnp.bfloat16)
    halves_ref[...] = jnp.concatenate([direction[:half], direction[half:]], axis=1)
    part = sources // 2
    spots = iota((cap * part, half), 1).astype(jnp.int16)

    def answer_part(p, carry):
        ids = message_ref[pl.ds(p * part * block + words, part, stride=block), :] - 1
        wanted = jnp.concatenate([jnp.broadcast_to(ids[:, s : s + 1], (part, lanes)) for s in range(cap)], axis=0)
        upper = wanted >= half
        spot = jnp.where(upper, wanted - half, wanted).astype(jnp.int16)
        hit = (spots == jnp.concatenate([spot] * (half // lanes), axis=1)).astype(jnp.bfloat16)
        both = dot(hit, halves_ref[...])
        found = jnp.where(upper, both[:, lanes:], both[:, :lanes])
        for s in range(cap):
            spread_ref[pl.ds(p * part * cap + s, part, stride=cap), :] = found[s * part : (s + 1) * part]
        rows = pl.ds(pl.multiple_of(p * part * cap, part * cap), part * cap)
        answer_ref[rows, :] = spread_ref[rows, :].astype(jnp.bfloat16)
        return carry

    lax.fori_loop(0, 2, answer_part, 0)
    for copy in copies:
        copy.wait()


def unpack_kernel(select_ref, back_ref, out_hbm, out_ref, out_sem):
    select = select_ref[...]
    slots = select.shape[1]
    copies = []
    for c in range(out_ref.shape[1] // LANES):
        columns = pl.ds(c * LANES, LANES)
        rows = dot(select, back_ref[c * slots : (c + 1) * slots])
        out_ref[:, columns] = rows.astype(jnp.bfloat16)
        copies.append(pltpu.make_async_copy(out_ref.at[:, columns], out_hbm.at[:, columns], out_sem.at[c]))
        copies[-1].start()
    for copy in copies:
        copy.wait()


VMEM = pl.BlockSpec(memory_space=pltpu.VMEM)
HBM = pl.BlockSpec(memory_space=pltpu.HBM)


def params_for(mib):
    return pltpu.CompilerParams(vmem_limit_bytes=mib * 1024 * 1024)


def local(grads, owners, local_ids, params, first_moment, second_moment, step_count):
    groups = lax.axis_size("rows")
    slices = lax.axis_size("cols")
    count, width = grads.shape
    own, lanes = params.shape
    cap = max(2, 2 * count // groups)
    block = cap // 2 + 1
    peers = groups * slices
    names = jnp.concatenate([owners.reshape(1, count), local_ids.reshape(1, count)], axis=0)
    message, select = pl.pallas_call(
        functools.partial(pack_kernel, groups, cap, own),
        out_shape=(
            jax.ShapeDtypeStruct((peers * block, lanes), jnp.int32),
            jax.ShapeDtypeStruct((count, groups * cap), jnp.bfloat16),
        ),
        in_specs=[VMEM, VMEM],
        out_specs=(VMEM, VMEM),
        compiler_params=params_for(40),
        name="pack",
    )(names, grads)
    message = message.reshape(peers, 1, block * lanes)
    message = lax.all_to_all(message, ORDER, split_axis=0, concat_axis=0, tiled=True)
    message = message.reshape(peers * block, lanes)
    table = jax.ShapeDtypeStruct((own, lanes), jnp.float32)
    new_params, new_first, new_second, answer = pl.pallas_call(
        functools.partial(update_kernel, cap),
        out_shape=(table, table, table, jax.ShapeDtypeStruct((peers * cap, lanes), jnp.bfloat16)),
        in_specs=[VMEM, VMEM, VMEM, VMEM, VMEM],
        out_specs=(HBM, HBM, HBM, VMEM),
        scratch_shapes=[
            pltpu.VMEM((peers * cap, lanes), jnp.float32),
            pltpu.VMEM((own // 2, 2 * lanes), jnp.bfloat16),
            pltpu.VMEM((3, own, lanes), jnp.float32),
            pltpu.SemaphoreType.DMA((3,)),
        ],
        compiler_params=params_for(48),
        name="update",
    )(message, step_count.reshape(1, 1), params, first_moment, second_moment)
    answer = answer.reshape(peers, cap, lanes)
    answer = lax.all_to_all(answer, ORDER, split_axis=0, concat_axis=0, tiled=True)
    row_steps = pl.pallas_call(
        unpack_kernel,
        out_shape=jax.ShapeDtypeStruct((count, width), jnp.bfloat16),
        in_specs=[VMEM, VMEM],
        out_specs=HBM,
        scratch_shapes=[pltpu.VMEM((count, width), jnp.bfloat16), pltpu.SemaphoreType.DMA((slices,))],
        compiler_params=params_for(40),
        name="unpack",
    )(select, answer.reshape(peers * cap, lanes))
    return (new_params, new_first, new_second, row_steps)


def solution(mesh):
    placed = (
        P(("rows", "cols"), None),
        P(("rows", "cols"), None),
        P(("rows", "cols")),
        P("rows", "cols"),
        P("rows", "cols"),
        P("rows", "cols"),
        P(),
    )
    return jax.shard_map(
        local,
        mesh=mesh,
        in_specs=placed,
        out_specs=(
            P("rows", "cols"),
            P("rows", "cols"),
            P("rows", "cols"),
            P(("rows", "cols"), None),
        ),
        check_vma=False,
    )
```

```python
import functools

import jax
import jax.numpy as jnp
import numpy as np
from jax import lax
from jax.experimental import pallas as pl
from jax.experimental.pallas import tpu as pltpu
from jax.sharding import PartitionSpec as P

LANES = 128
FULL = 32767.0
ORDER = ("cols", "rows")


def iota(shape, axis):
    return lax.broadcasted_iota(jnp.int32, shape, axis)


def dot(a, b):
    return jnp.dot(a, b, preferred_element_type=jnp.float32)


def dot_nt(a, b):
    return lax.dot_general(a, b, (((1,), (1,)), ((), ())), preferred_element_type=jnp.float32)


def one_minus_power(base, steps):
    factor = 1.0 - float(np.float32(base))
    total = jnp.zeros_like(steps, jnp.float32)
    for bit in range(5):
        has = ((steps >> bit) & 1).astype(jnp.float32)
        total = total + has * np.float32(factor) * (1.0 - total)
        factor = factor * (2.0 - factor)
    return total


def pack_kernel(
    groups, cap, owners_hbm, ids_hbm, grads_hbm, message_hbm, select_hbm,
    owners_ref, ids_ref, grads_ref, message_ref, select_ref, names_sem, grads_sem, message_sem, select_sem,
):
    count, width = grads_ref.shape
    words = cap // 2
    block = words + 1
    slices = width // LANES
    share = groups * block
    names = [
        pltpu.make_async_copy(owners_hbm, owners_ref, names_sem.at[0]),
        pltpu.make_async_copy(ids_hbm, ids_ref, names_sem.at[1]),
    ]
    load = pltpu.make_async_copy(grads_hbm, grads_ref, grads_sem)
    for copy in names:
        copy.start()
    load.start()
    for copy in names:
        copy.wait()

    owner = owners_ref[...]
    mine = owner == iota((groups, count), 0)
    mine_half = mine.astype(jnp.bfloat16)
    square = (count, count)
    earlier = (iota(square, 0) < iota(square, 1)).astype(jnp.bfloat16)
    before = jnp.where(mine, dot(mine_half, earlier), 0.0)
    position = jnp.sum(before, axis=0, keepdims=True).astype(jnp.int32)
    place = (iota((groups * cap, count), 0) == position * groups + owner).astype(jnp.bfloat16)
    on_diagonal = iota(square, 0) == iota(square, 1)

    target = (owner * cap + position).astype(jnp.float32)
    target = jnp.sum(jnp.where(on_diagonal, target, 0.0), axis=1, keepdims=True).astype(jnp.int32)
    select_ref[...] = (iota((count, groups * cap), 1) == target).astype(jnp.bfloat16)
    stores = [pltpu.make_async_copy(select_ref, select_hbm, select_sem)]
    stores[0].start()

    load.wait()
    grads = grads_ref[...]
    size = jnp.abs(grads)
    top = jnp.max(size, axis=1, keepdims=True)
    power = jnp.clip(jnp.ceil(jnp.log2(top)), -120.0, 100.0)
    code = jnp.minimum(jnp.floor(jnp.sqrt(size * jnp.exp2(-power)) * FULL + 0.5), FULL)
    code = jnp.where(grads < 0.0, -code, code)
    high = jnp.floor(code * (1.0 / 256.0) + 0.5)
    low = (code - high * 256.0).astype(jnp.bfloat16)
    high = high.astype(jnp.bfloat16)

    power_row = jnp.sum(jnp.where(on_diagonal, power, 0.0), axis=0, keepdims=True)
    named = ids_ref[...] + 1
    lane = iota((LANES, count), 0)
    at_id = lane == position
    at_power = lane == position + cap
    facts_high = jnp.where(at_id, lax.div(named, 32).astype(jnp.float32), 0.0).astype(jnp.bfloat16)
    facts_low = jnp.where(at_id, lax.rem(named, 32).astype(jnp.float32), jnp.where(at_power, power_row, 0.0))
    facts = dot_nt(mine_half, facts_high) * 32.0 + dot_nt(mine_half, facts_low.astype(jnp.bfloat16))
    facts = facts.astype(jnp.int32)

    for c in range(slices):
        columns = slice(c * LANES, (c + 1) * LANES)
        placed = dot(place, jnp.concatenate([high[:, columns], low[:, columns]], axis=1))
        placed = (placed[:, :LANES] * 256.0 + placed[:, LANES:]).astype(jnp.int32)
        for j in range(words):
            one = placed[j * groups : (j + 1) * groups]
            two = placed[(j + words) * groups : (j + words + 1) * groups]
            message_ref[pl.ds(c * share + j, groups, stride=block), :] = (one & 0xFFFF) | (two << 16)
        message_ref[pl.ds(c * share + words, groups, stride=block), :] = facts
        rows = pl.ds(c * share, share)
        stores.append(pltpu.make_async_copy(message_ref.at[rows], message_hbm.at[rows], message_sem.at[c]))
        stores[-1].start()

    for copy in stores:
        copy.wait()


def update_kernel(
    cap, message_ref, step_ref, params_ref, first_ref, second_ref,
    new_params_hbm, new_first_hbm, new_second_hbm, answer_ref, spread_ref, halves_ref, table_ref, table_sem,
):
    own, lanes = params_ref.shape
    words = cap // 2
    block = words + 1
    sources = message_ref.shape[0] // block
    facts = message_ref[pl.ds(words, sources, stride=block), :]
    across = facts.astype(jnp.float32).T
    id_rows = across[:cap].astype(jnp.int32) - 1
    scale_rows = jnp.exp2(across[cap : 2 * cap]).astype(jnp.bfloat16)
    short_rows = id_rows.astype(jnp.int16)
    items = iota((own, sources), 0).astype(jnp.int16)
    total = jnp.zeros((own, 2 * lanes), jnp.float32)
    for j in range(words):
        word = message_ref[pl.ds(j, sources, stride=block), :]
        for s, code in ((j, (word << 16) >> 16), (j + words, word >> 16)):
            code = code.astype(jnp.float32)
            value = code * jnp.abs(code)
            high = value.astype(jnp.bfloat16)
            low = (value - high.astype(jnp.float32)).astype(jnp.bfloat16)
            hit = jnp.where(items == short_rows[s : s + 1], scale_rows[s : s + 1], jnp.bfloat16(0))
            total = total + dot(hit, jnp.concatenate([high, low], axis=1))
    fine = 32
    coarse = own // fine
    counts = jnp.zeros((coarse, fine), jnp.float32)
    for s in range(cap):
        row = id_rows[s : s + 1]
        whole = (iota((coarse, sources), 0) == lax.div(row, fine)).astype(jnp.bfloat16)
        rest = (iota((fine, sources), 0) == lax.rem(row, fine)).astype(jnp.bfloat16)
        counts = counts + dot_nt(whole, rest)
    counts = jnp.minimum(counts, 1.0).astype(jnp.bfloat16)
    whole = (lax.div(iota((own, coarse), 0), fine) == iota((own, coarse), 1)).astype(jnp.bfloat16)
    rest = lax.rem(iota((own, fine), 0), fine) == iota((own, fine), 1)
    live = jnp.sum(jnp.where(rest, dot(whole, counts), 0.0), axis=1, keepdims=True) > 0.0
    summed = (total[:, :lanes] + total[:, lanes:]) * (1.0 / (FULL * FULL))
    fix_first = one_minus_power(0.9, step_ref[...])
    fix_second = one_minus_power(0.999, step_ref[...])
    first, second, params = first_ref[...], second_ref[...], params_ref[...]
    new_first = jnp.where(live, 0.9 * first + 0.1 * summed, first)
    new_second = jnp.where(live, 0.999 * second + 0.001 * summed * summed, second)
    direction = -(new_first / fix_first) / (jnp.sqrt(new_second / fix_second) + 1e-08)
    table_ref[0] = jnp.where(live, params + 0.01 * direction, params)
    table_ref[1] = new_first
    table_ref[2] = new_second
    copies = [
        pltpu.make_async_copy(table_ref.at[n], out, table_sem.at[n])
        for n, out in enumerate((new_params_hbm, new_first_hbm, new_second_hbm))
    ]
    for copy in copies:
        copy.start()

    half = own // 2
    direction = direction.astype(jnp.bfloat16)
    halves_ref[...] = jnp.concatenate([direction[:half], direction[half:]], axis=1)
    part = sources // 2
    spots = iota((cap * part, half), 1).astype(jnp.int16)

    def answer_part(p, carry):
        ids = message_ref[pl.ds(p * part * block + words, part, stride=block), :] - 1
        wanted = jnp.concatenate([jnp.broadcast_to(ids[:, s : s + 1], (part, lanes)) for s in range(cap)], axis=0)
        upper = wanted >= half
        spot = jnp.where(upper, wanted - half, wanted).astype(jnp.int16)
        hit = (spots == jnp.concatenate([spot] * (half // lanes), axis=1)).astype(jnp.bfloat16)
        both = dot(hit, halves_ref[...])
        found = jnp.where(upper, both[:, lanes:], both[:, :lanes])
        for s in range(cap):
            spread_ref[pl.ds(p * part * cap + s, part, stride=cap), :] = found[s * part : (s + 1) * part]
        rows = pl.ds(pl.multiple_of(p * part * cap, part * cap), part * cap)
        answer_ref[rows, :] = spread_ref[rows, :].astype(jnp.bfloat16)
        return carry

    lax.fori_loop(0, 2, answer_part, 0)
    for copy in copies:
        copy.wait()


def unpack_kernel(select_ref, back_ref, out_hbm, out_ref, out_sem):
    select = select_ref[...]
    slots = select.shape[1]
    copies = []
    for c in range(out_ref.shape[1] // LANES):
        columns = pl.ds(c * LANES, LANES)
        rows = dot(select, back_ref[c * slots : (c + 1) * slots])
        out_ref[:, columns] = rows.astype(jnp.bfloat16)
        copies.append(pltpu.make_async_copy(out_ref.at[:, columns], out_hbm.at[:, columns], out_sem.at[c]))
        copies[-1].start()
    for copy in copies:
        copy.wait()


VMEM = pl.BlockSpec(memory_space=pltpu.VMEM)
HBM = pl.BlockSpec(memory_space=pltpu.HBM)


def params_for(mib):
    return pltpu.CompilerParams(vmem_limit_bytes=mib * 1024 * 1024)


def local(grads, owners, local_ids, params, first_moment, second_moment, step_count):
    groups = lax.axis_size("rows")
    slices = lax.axis_size("cols")
    count, width = grads.shape
    own, lanes = params.shape
    cap = max(2, 2 * count // groups)
    block = cap // 2 + 1
    peers = groups * slices
    message, select = pl.pallas_call(
        functools.partial(pack_kernel, groups, cap),
        out_shape=(
            jax.ShapeDtypeStruct((peers * block, lanes), jnp.int32),
            jax.ShapeDtypeStruct((count, groups * cap), jnp.bfloat16),
        ),
        in_specs=[HBM, HBM, HBM],
        out_specs=(HBM, HBM),
        scratch_shapes=[
            pltpu.VMEM((1, count), jnp.int32),
            pltpu.VMEM((1, count), jnp.int32),
            pltpu.VMEM((count, width), jnp.float32),
            pltpu.VMEM((peers * block, lanes), jnp.int32),
            pltpu.VMEM((count, groups * cap), jnp.bfloat16),
            pltpu.SemaphoreType.DMA((2,)),
            pltpu.SemaphoreType.DMA,
            pltpu.SemaphoreType.DMA((slices,)),
            pltpu.SemaphoreType.DMA,
        ],
        compiler_params=params_for(56),
        name="pack",
    )(owners.reshape(1, count), local_ids.reshape(1, count), grads)
    message = message.reshape(peers, 1, block * lanes)
    message = lax.all_to_all(message, ORDER, split_axis=0, concat_axis=0, tiled=True)
    message = message.reshape(peers * block, lanes)
    table = jax.ShapeDtypeStruct((own, lanes), jnp.float32)
    new_params, new_first, new_second, answer = pl.pallas_call(
        functools.partial(update_kernel, cap),
        out_shape=(table, table, table, jax.ShapeDtypeStruct((peers * cap, lanes), jnp.bfloat16)),
        in_specs=[VMEM, VMEM, VMEM, VMEM, VMEM],
        out_specs=(HBM, HBM, HBM, VMEM),
        scratch_shapes=[
            pltpu.VMEM((peers * cap, lanes), jnp.float32),
            pltpu.VMEM((own // 2, 2 * lanes), jnp.bfloat16),
            pltpu.VMEM((3, own, lanes), jnp.float32),
            pltpu.SemaphoreType.DMA((3,)),
        ],
        compiler_params=params_for(48),
        name="update",
    )(message, step_count.reshape(1, 1), params, first_moment, second_moment)
    answer = answer.reshape(peers, cap, lanes)
    answer = lax.all_to_all(answer, ORDER, split_axis=0, concat_axis=0, tiled=True)
    row_steps = pl.pallas_call(
        unpack_kernel,
        out_shape=jax.ShapeDtypeStruct((count, width), jnp.bfloat16),
        in_specs=[VMEM, VMEM],
        out_specs=HBM,
        scratch_shapes=[pltpu.VMEM((count, width), jnp.bfloat16), pltpu.SemaphoreType.DMA((slices,))],
        compiler_params=params_for(40),
        name="unpack",
    )(select, answer.reshape(peers * cap, lanes))
    return (new_params, new_first, new_second, row_steps)


def solution(mesh):
    placed = (
        P(("rows", "cols"), None),
        P(("rows", "cols"), None),
        P(("rows", "cols")),
        P("rows", "cols"),
        P("rows", "cols"),
        P("rows", "cols"),
        P(),
    )
    return jax.shard_map(
        local,
        mesh=mesh,
        in_specs=placed,
        out_specs=(
            P("rows", "cols"),
            P("rows", "cols"),
            P("rows", "cols"),
            P(("rows", "cols"), None),
        ),
        check_vma=False,
    )
```

```python
import functools

import jax
import jax.numpy as jnp
import numpy as np
from jax import lax
from jax.experimental import pallas as pl
from jax.experimental.pallas import tpu as pltpu
from jax.sharding import PartitionSpec as P

LANES = 128
FULL = 32767.0
TINY = 1e-30
SPARE = 8
ORDER = ("cols", "rows")


def iota(shape, axis):
    return lax.broadcasted_iota(jnp.int32, shape, axis)


def dot(a, b):
    return jnp.dot(a, b, preferred_element_type=jnp.float32)


def dot_nt(a, b):
    return lax.dot_general(a, b, (((1,), (1,)), ((), ())), preferred_element_type=jnp.float32)


def one_minus_power(base, steps):
    factor = 1.0 - float(np.float32(base))
    total = jnp.zeros_like(steps, jnp.float32)
    for bit in range(5):
        has = ((steps >> bit) & 1).astype(jnp.float32)
        total = total + has * np.float32(factor) * (1.0 - total)
        factor = factor * (2.0 - factor)
    return total


def pack_kernel(
    groups, cap, owners_hbm, ids_hbm, grads_hbm, message_hbm, select_hbm,
    owners_ref, ids_ref, grads_ref, message_ref, select_ref, names_sem, grads_sem, message_sem, select_sem,
):
    count, width = grads_ref.shape
    words = cap // 2
    block = words + 1
    slices = width // LANES
    share = groups * block
    names = [
        pltpu.make_async_copy(owners_hbm, owners_ref, names_sem.at[0]),
        pltpu.make_async_copy(ids_hbm, ids_ref, names_sem.at[1]),
    ]
    load = pltpu.make_async_copy(grads_hbm, grads_ref, grads_sem)
    for copy in names:
        copy.start()
    load.start()
    for copy in names:
        copy.wait()

    owner = owners_ref[...]
    mine = owner == iota((groups, count), 0)
    mine_half = mine.astype(jnp.bfloat16)
    square = (count, count)
    earlier = (iota(square, 0) < iota(square, 1)).astype(jnp.bfloat16)
    before = jnp.where(mine, dot(mine_half, earlier), 0.0)
    position = jnp.sum(before, axis=0, keepdims=True).astype(jnp.int32)
    place = (iota((groups * cap, count), 0) == position * groups + owner).astype(jnp.bfloat16)
    on_diagonal = iota(square, 0) == iota(square, 1)

    target = (owner * cap + position).astype(jnp.float32)
    target = jnp.sum(jnp.where(on_diagonal, target, 0.0), axis=1, keepdims=True).astype(jnp.int32)
    select_ref[...] = (iota((count, groups * cap), 1) == target).astype(jnp.bfloat16)
    stores = [pltpu.make_async_copy(select_ref, select_hbm, select_sem)]
    stores[0].start()

    load.wait()
    grads = grads_ref[...]
    size = jnp.abs(grads)
    top = jnp.max(size, axis=1, keepdims=True)
    power = jnp.ceil(jnp.log2(jnp.maximum(top, TINY)))
    code = jnp.minimum(jnp.floor(jnp.sqrt(size * jnp.exp2(-power)) * FULL + 0.5), FULL)
    code = jnp.where(grads < 0.0, -code, code)
    high = jnp.floor(code * (1.0 / 256.0) + 0.5)
    low = (code - high * 256.0).astype(jnp.bfloat16)
    high = high.astype(jnp.bfloat16)

    power_row = jnp.sum(jnp.where(on_diagonal, power, 0.0), axis=0, keepdims=True)
    named = ids_ref[...] + 1
    lane = iota((LANES, count), 0)
    at_id = lane == position
    at_power = lane == position + cap
    facts_high = jnp.where(at_id, lax.div(named, 32).astype(jnp.float32), 0.0).astype(jnp.bfloat16)
    facts_low = jnp.where(at_id, lax.rem(named, 32).astype(jnp.float32), jnp.where(at_power, power_row, 0.0))
    facts = dot_nt(mine_half, facts_high) * 32.0 + dot_nt(mine_half, facts_low.astype(jnp.bfloat16))
    facts = facts.astype(jnp.int32)

    for c in range(slices):
        columns = slice(c * LANES, (c + 1) * LANES)
        placed = dot(place, jnp.concatenate([high[:, columns], low[:, columns]], axis=1))
        placed = (placed[:, :LANES] * 256.0 + placed[:, LANES:]).astype(jnp.int32)
        for j in range(words):
            one = placed[j * groups : (j + 1) * groups]
            two = placed[(j + words) * groups : (j + words + 1) * groups]
            message_ref[pl.ds(c * share + j, groups, stride=block), :] = (one & 0xFFFF) | (two << 16)
        message_ref[pl.ds(c * share + words, groups, stride=block), :] = facts
        rows = pl.ds(c * share, share)
        stores.append(pltpu.make_async_copy(message_ref.at[rows], message_hbm.at[rows], message_sem.at[c]))
        stores[-1].start()

    for copy in stores:
        copy.wait()


def update_kernel(
    cap, message_ref, step_ref, params_ref, first_ref, second_ref,
    new_params_hbm, new_first_hbm, new_second_hbm, answer_ref,
    tail_ref, facts_ref, spread_ref, halves_ref, table_ref, table_sem,
):
    own, lanes = params_ref.shape
    words = cap // 2
    block = words + 1
    sources = message_ref.shape[0] // block
    tail = SPARE * block
    tail_ref[:tail] = message_ref[sources * block - tail :]

    def row(j):
        most = message_ref[pl.ds(j, sources - SPARE, stride=block), :]
        return jnp.concatenate([most, tail_ref[pl.ds(j, SPARE, stride=block), :]], axis=0)

    facts = row(words)
    facts_ref[...] = facts
    across = facts.astype(jnp.float32).T
    id_rows = across[:cap].astype(jnp.int32) - 1
    scale_rows = jnp.exp2(across[cap : 2 * cap]).astype(jnp.bfloat16)
    short_rows = id_rows.astype(jnp.int16)
    items = iota((own, sources), 0).astype(jnp.int16)
    total = jnp.zeros((own, 2 * lanes), jnp.float32)
    for j in range(words):
        word = row(j)
        for s, code in ((j, (word << 16) >> 16), (j + words, word >> 16)):
            code = code.astype(jnp.float32)
            value = code * jnp.abs(code)
            high = value.astype(jnp.bfloat16)
            low = (value - high.astype(jnp.float32)).astype(jnp.bfloat16)
            hit = jnp.where(items == short_rows[s : s + 1], scale_rows[s : s + 1], jnp.bfloat16(0))
            total = total + dot(hit, jnp.concatenate([high, low], axis=1))
    fine = 32
    coarse = own // fine
    counts = jnp.zeros((coarse, fine), jnp.float32)
    for s in range(cap):
        ids = id_rows[s : s + 1]
        whole = (iota((coarse, sources), 0) == lax.div(ids, fine)).astype(jnp.bfloat16)
        rest = (iota((fine, sources), 0) == lax.rem(ids, fine)).astype(jnp.bfloat16)
        counts = counts + dot_nt(whole, rest)
    counts = jnp.minimum(counts, 1.0).astype(jnp.bfloat16)
    whole = (lax.div(iota((own, coarse), 0), fine) == iota((own, coarse), 1)).astype(jnp.bfloat16)
    rest = lax.rem(iota((own, fine), 0), fine) == iota((own, fine), 1)
    live = jnp.sum(jnp.where(rest, dot(whole, counts), 0.0), axis=1, keepdims=True) > 0.0
    summed = (total[:, :lanes] + total[:, lanes:]) * (1.0 / (FULL * FULL))
    fix_first = one_minus_power(0.9, step_ref[...])
    fix_second = one_minus_power(0.999, step_ref[...])
    first, second, params = first_ref[...], second_ref[...], params_ref[...]
    new_first = jnp.where(live, 0.9 * first + 0.1 * summed, first)
    new_second = jnp.where(live, 0.999 * second + 0.001 * summed * summed, second)
    direction = -(new_first / fix_first) / (jnp.sqrt(new_second / fix_second) + 1e-08)
    table_ref[0] = jnp.where(live, params + 0.01 * direction, params)
    table_ref[1] = new_first
    table_ref[2] = new_second
    copies = [
        pltpu.make_async_copy(table_ref.at[n], out, table_sem.at[n])
        for n, out in enumerate((new_params_hbm, new_first_hbm, new_second_hbm))
    ]
    for copy in copies:
        copy.start()

    half = own // 2
    direction = direction.astype(jnp.bfloat16)
    halves_ref[...] = jnp.concatenate([direction[:half], direction[half:]], axis=1)
    part = sources // 2
    spots = iota((cap * part, half), 1).astype(jnp.int16)

    def answer_part(p, carry):
        ids = facts_ref[pl.ds(pl.multiple_of(p * part, part), part), :] - 1
        wanted = jnp.concatenate([jnp.broadcast_to(ids[:, s : s + 1], (part, lanes)) for s in range(cap)], axis=0)
        upper = wanted >= half
        spot = jnp.where(upper, wanted - half, wanted).astype(jnp.int16)
        hit = (spots == jnp.concatenate([spot] * (half // lanes), axis=1)).astype(jnp.bfloat16)
        both = dot(hit, halves_ref[...])
        found = jnp.where(upper, both[:, lanes:], both[:, :lanes])
        for s in range(cap):
            spread_ref[pl.ds(s, part, stride=cap), :] = found[s * part : (s + 1) * part]
        rows = pl.ds(pl.multiple_of(p * part * cap, part * cap), part * cap)
        answer_ref[rows, :] = spread_ref[: part * cap].astype(jnp.bfloat16)
        return carry

    lax.fori_loop(0, 2, answer_part, 0)
    for copy in copies:
        copy.wait()


def unpack_kernel(select_ref, back_ref, out_hbm, out_ref, out_sem):
    select = select_ref[...]
    slots = select.shape[1]
    copies = []
    for c in range(out_ref.shape[1] // LANES):
        columns = pl.ds(c * LANES, LANES)
        rows = dot(select, back_ref[c * slots : (c + 1) * slots])
        out_ref[:, columns] = rows.astype(jnp.bfloat16)
        copies.append(pltpu.make_async_copy(out_ref.at[:, columns], out_hbm.at[:, columns], out_sem.at[c]))
        copies[-1].start()
    for copy in copies:
        copy.wait()


VMEM = pl.BlockSpec(memory_space=pltpu.VMEM)
HBM = pl.BlockSpec(memory_space=pltpu.HBM)


def params_for(mib):
    return pltpu.CompilerParams(vmem_limit_bytes=mib * 1024 * 1024)


def local(grads, owners, local_ids, params, first_moment, second_moment, step_count):
    groups = lax.axis_size("rows")
    slices = lax.axis_size("cols")
    count, width = grads.shape
    own, lanes = params.shape
    cap = max(2, 2 * count // groups)
    block = cap // 2 + 1
    peers = groups * slices
    message, select = pl.pallas_call(
        functools.partial(pack_kernel, groups, cap),
        out_shape=(
            jax.ShapeDtypeStruct((peers * block, lanes), jnp.int32),
            jax.ShapeDtypeStruct((count, groups * cap), jnp.bfloat16),
        ),
        in_specs=[HBM, HBM, HBM],
        out_specs=(HBM, HBM),
        scratch_shapes=[
            pltpu.VMEM((1, count), jnp.int32),
            pltpu.VMEM((1, count), jnp.int32),
            pltpu.VMEM((count, width), jnp.float32),
            pltpu.VMEM((peers * block + SPARE, lanes), jnp.int32),
            pltpu.VMEM((count, groups * cap), jnp.bfloat16),
            pltpu.SemaphoreType.DMA((2,)),
            pltpu.SemaphoreType.DMA,
            pltpu.SemaphoreType.DMA((slices,)),
            pltpu.SemaphoreType.DMA,
        ],
        compiler_params=params_for(56),
        name="pack",
    )(owners.reshape(1, count), local_ids.reshape(1, count), grads)
    message = message.reshape(peers, 1, block * lanes)
    message = lax.all_to_all(message, ORDER, split_axis=0, concat_axis=0, tiled=True)
    message = message.reshape(peers * block, lanes)
    table = jax.ShapeDtypeStruct((own, lanes), jnp.float32)
    new_params, new_first, new_second, answer = pl.pallas_call(
        functools.partial(update_kernel, cap),
        out_shape=(table, table, table, jax.ShapeDtypeStruct((peers * cap, lanes), jnp.bfloat16)),
        in_specs=[VMEM, VMEM, VMEM, VMEM, VMEM],
        out_specs=(HBM, HBM, HBM, VMEM),
        scratch_shapes=[
            pltpu.VMEM((SPARE * block + SPARE, lanes), jnp.int32),
            pltpu.VMEM((peers, lanes), jnp.int32),
            pltpu.VMEM((peers * cap // 2 + SPARE, lanes), jnp.float32),
            pltpu.VMEM((own // 2, 2 * lanes), jnp.bfloat16),
            pltpu.VMEM((3, own, lanes), jnp.float32),
            pltpu.SemaphoreType.DMA((3,)),
        ],
        compiler_params=params_for(48),
        name="update",
    )(message, step_count.reshape(1, 1), params, first_moment, second_moment)
    answer = answer.reshape(peers, cap, lanes)
    answer = lax.all_to_all(answer, ORDER, split_axis=0, concat_axis=0, tiled=True)
    row_steps = pl.pallas_call(
        unpack_kernel,
        out_shape=jax.ShapeDtypeStruct((count, width), jnp.bfloat16),
        in_specs=[VMEM, VMEM],
        out_specs=HBM,
        scratch_shapes=[pltpu.VMEM((count, width), jnp.bfloat16), pltpu.SemaphoreType.DMA((slices,))],
        compiler_params=params_for(40),
        name="unpack",
    )(select, answer.reshape(peers * cap, lanes))
    return (new_params, new_first, new_second, row_steps)


def solution(mesh):
    placed = (
        P(("rows", "cols"), None),
        P(("rows", "cols"), None),
        P(("rows", "cols")),
        P("rows", "cols"),
        P("rows", "cols"),
        P("rows", "cols"),
        P(),
    )
    return jax.shard_map(
        local,
        mesh=mesh,
        in_specs=placed,
        out_specs=(
            P("rows", "cols"),
            P("rows", "cols"),
            P("rows", "cols"),
            P(("rows", "cols"), None),
        ),
        check_vma=False,
    )
```

```python
import functools

import jax
import jax.numpy as jnp
import numpy as np
from jax import lax
from jax.experimental import pallas as pl
from jax.experimental.pallas import tpu as pltpu
from jax.sharding import PartitionSpec as P

LANES = 128
FULL = 32767.0
TINY = 1e-30
SPARE = 8
ORDER = ("cols", "rows")


def iota(shape, axis):
    return lax.broadcasted_iota(jnp.int32, shape, axis)


def dot(a, b):
    return jnp.dot(a, b, preferred_element_type=jnp.float32)


def dot_nt(a, b):
    return lax.dot_general(a, b, (((1,), (1,)), ((), ())), preferred_element_type=jnp.float32)


def one_minus_power(base, steps):
    factor = 1.0 - float(np.float32(base))
    total = jnp.zeros_like(steps, jnp.float32)
    for bit in range(5):
        has = ((steps >> bit) & 1).astype(jnp.float32)
        total = total + has * np.float32(factor) * (1.0 - total)
        factor = factor * (2.0 - factor)
    return total


def pack_kernel(
    groups, cap, owners_hbm, ids_hbm, grads_hbm, message_hbm, select_hbm,
    owners_ref, ids_ref, grads_ref, message_ref, select_ref, names_sem, grads_sem, message_sem, select_sem,
):
    count, width = grads_ref.shape
    words = cap // 2
    block = words + 1
    slices = width // LANES
    share = groups * block
    names = [
        pltpu.make_async_copy(owners_hbm, owners_ref, names_sem.at[0]),
        pltpu.make_async_copy(ids_hbm, ids_ref, names_sem.at[1]),
    ]
    load = pltpu.make_async_copy(grads_hbm, grads_ref, grads_sem)
    for copy in names:
        copy.start()
    load.start()
    for copy in names:
        copy.wait()

    owner = owners_ref[...]
    mine = owner == iota((groups, count), 0)
    mine_half = mine.astype(jnp.bfloat16)
    square = (count, count)
    earlier = (iota(square, 0) < iota(square, 1)).astype(jnp.bfloat16)
    before = jnp.where(mine, dot(mine_half, earlier), 0.0)
    position = jnp.sum(before, axis=0, keepdims=True).astype(jnp.int32)
    place = (iota((groups * cap, count), 0) == position * groups + owner).astype(jnp.bfloat16)
    on_diagonal = iota(square, 0) == iota(square, 1)

    target = (owner * cap + position).astype(jnp.float32)
    target = jnp.sum(jnp.where(on_diagonal, target, 0.0), axis=1, keepdims=True).astype(jnp.int32)
    select_ref[...] = (iota((count, groups * cap), 1) == target).astype(jnp.bfloat16)
    stores = [pltpu.make_async_copy(select_ref, select_hbm, select_sem)]
    stores[0].start()

    named = ids_ref[...] + 1
    lane = iota((LANES, count), 0)
    at_id = lane == position
    at_power = lane == position + cap
    names_high = jnp.where(at_id, lax.div(named, 32).astype(jnp.float32), 0.0).astype(jnp.bfloat16)
    names_low = jnp.where(at_id, lax.rem(named, 32).astype(jnp.float32), 0.0).astype(jnp.bfloat16)
    facts = dot_nt(mine_half, names_high) * 32.0 + dot_nt(mine_half, names_low)

    load.wait()
    grads = grads_ref[...]
    size = jnp.abs(grads)
    top = jnp.max(size, axis=1, keepdims=True)
    power = jnp.ceil(jnp.log2(jnp.maximum(top, TINY)))
    code = jnp.minimum(jnp.floor(jnp.sqrt(size * jnp.exp2(-power)) * FULL + 0.5), FULL)
    code = jnp.where(grads < 0.0, -code, code)
    high = jnp.floor(code * (1.0 / 256.0) + 0.5)
    low = (code - high * 256.0).astype(jnp.bfloat16)
    high = high.astype(jnp.bfloat16)

    power_row = jnp.sum(jnp.where(on_diagonal, power, 0.0), axis=0, keepdims=True)
    powers = jnp.where(at_power, power_row, 0.0).astype(jnp.bfloat16)
    facts = (facts + dot_nt(mine_half, powers)).astype(jnp.int32)

    for c in range(slices):
        columns = slice(c * LANES, (c + 1) * LANES)
        placed = dot(place, jnp.concatenate([high[:, columns], low[:, columns]], axis=1))
        placed = (placed[:, :LANES] * 256.0 + placed[:, LANES:]).astype(jnp.int32)
        for j in range(words):
            one = placed[j * groups : (j + 1) * groups]
            two = placed[(j + words) * groups : (j + words + 1) * groups]
            message_ref[pl.ds(c * share + j, groups, stride=block), :] = (one & 0xFFFF) | (two << 16)
        message_ref[pl.ds(c * share + words, groups, stride=block), :] = facts
        rows = pl.ds(c * share, share)
        stores.append(pltpu.make_async_copy(message_ref.at[rows], message_hbm.at[rows], message_sem.at[c]))
        stores[-1].start()

    for copy in stores:
        copy.wait()


def update_kernel(
    cap, message_ref, step_ref, params_ref, first_ref, second_ref,
    new_params_hbm, new_first_hbm, new_second_hbm, answer_ref,
    tail_ref, facts_ref, spread_ref, halves_ref, table_ref, table_sem,
):
    own, lanes = params_ref.shape
    words = cap // 2
    block = words + 1
    sources = message_ref.shape[0] // block
    tail = SPARE * block
    tail_ref[:tail] = message_ref[sources * block - tail :]

    def row(j):
        most = message_ref[pl.ds(j, sources - SPARE, stride=block), :]
        return jnp.concatenate([most, tail_ref[pl.ds(j, SPARE, stride=block), :]], axis=0)

    facts = row(words)
    facts_ref[...] = facts
    across = facts.astype(jnp.float32).T
    id_rows = across[:cap].astype(jnp.int32) - 1
    scale_rows = jnp.exp2(across[cap : 2 * cap]).astype(jnp.bfloat16)
    short_rows = id_rows.astype(jnp.int16)
    fine = 32
    coarse = own // fine
    counts = jnp.zeros((coarse, fine), jnp.float32)
    for s in range(cap):
        ids = id_rows[s : s + 1]
        whole = (iota((coarse, sources), 0) == lax.div(ids, fine)).astype(jnp.bfloat16)
        rest = (iota((fine, sources), 0) == lax.rem(ids, fine)).astype(jnp.bfloat16)
        counts = counts + dot_nt(whole, rest)
    counts = jnp.minimum(counts, 1.0).astype(jnp.bfloat16)
    whole = (lax.div(iota((own, coarse), 0), fine) == iota((own, coarse), 1)).astype(jnp.bfloat16)
    rest = lax.rem(iota((own, fine), 0), fine) == iota((own, fine), 1)
    live = jnp.sum(jnp.where(rest, dot(whole, counts), 0.0), axis=1, keepdims=True) > 0.0
    items = iota((own, sources), 0).astype(jnp.int16)
    total = jnp.zeros((own, 2 * lanes), jnp.float32)
    for j in range(words):
        word = row(j)
        for s, code in ((j, (word << 16) >> 16), (j + words, word >> 16)):
            code = code.astype(jnp.float32)
            value = code * jnp.abs(code)
            high = value.astype(jnp.bfloat16)
            low = (value - high.astype(jnp.float32)).astype(jnp.bfloat16)
            hit = jnp.where(items == short_rows[s : s + 1], scale_rows[s : s + 1], jnp.bfloat16(0))
            total = total + dot(hit, jnp.concatenate([high, low], axis=1))
    summed = (total[:, :lanes] + total[:, lanes:]) * (1.0 / (FULL * FULL))
    fix_first = one_minus_power(0.9, step_ref[...])
    fix_second = one_minus_power(0.999, step_ref[...])
    first, second, params = first_ref[...], second_ref[...], params_ref[...]
    new_first = jnp.where(live, 0.9 * first + 0.1 * summed, first)
    new_second = jnp.where(live, 0.999 * second + 0.001 * summed * summed, second)
    direction = -(new_first / fix_first) / (jnp.sqrt(new_second / fix_second) + 1e-08)
    table_ref[0] = jnp.where(live, params + 0.01 * direction, params)
    table_ref[1] = new_first
    table_ref[2] = new_second
    copies = [
        pltpu.make_async_copy(table_ref.at[n], out, table_sem.at[n])
        for n, out in enumerate((new_params_hbm, new_first_hbm, new_second_hbm))
    ]
    for copy in copies:
        copy.start()

    half = own // 2
    direction = direction.astype(jnp.bfloat16)
    halves_ref[...] = jnp.concatenate([direction[:half], direction[half:]], axis=1)
    part = sources // 2
    spots = iota((cap * part, half), 1).astype(jnp.int16)

    def answer_part(p, carry):
        ids = facts_ref[pl.ds(pl.multiple_of(p * part, part), part), :] - 1
        wanted = jnp.concatenate([jnp.broadcast_to(ids[:, s : s + 1], (part, lanes)) for s in range(cap)], axis=0)
        upper = wanted >= half
        spot = jnp.where(upper, wanted - half, wanted).astype(jnp.int16)
        hit = (spots == jnp.concatenate([spot] * (half // lanes), axis=1)).astype(jnp.bfloat16)
        both = dot(hit, halves_ref[...])
        found = jnp.where(upper, both[:, lanes:], both[:, :lanes])
        for s in range(cap):
            spread_ref[pl.ds(s, part, stride=cap), :] = found[s * part : (s + 1) * part]
        rows = pl.ds(pl.multiple_of(p * part * cap, part * cap), part * cap)
        answer_ref[rows, :] = spread_ref[: part * cap].astype(jnp.bfloat16)
        return carry

    lax.fori_loop(0, 2, answer_part, 0)
    for copy in copies:
        copy.wait()


def unpack_kernel(select_ref, back_ref, out_hbm, out_ref, out_sem):
    select = select_ref[...]
    slots = select.shape[1]
    copies = []
    for c in range(0, out_ref.shape[1] // LANES, 2):
        columns = pl.ds(c * LANES, 2 * LANES)
        one, two = back_ref[c * slots : (c + 1) * slots], back_ref[(c + 1) * slots : (c + 2) * slots]
        out_ref[:, columns] = dot(select, jnp.concatenate([one, two], axis=1)).astype(jnp.bfloat16)
        copies.append(pltpu.make_async_copy(out_ref.at[:, columns], out_hbm.at[:, columns], out_sem.at[c // 2]))
        copies[-1].start()
    for copy in copies:
        copy.wait()


VMEM = pl.BlockSpec(memory_space=pltpu.VMEM)
HBM = pl.BlockSpec(memory_space=pltpu.HBM)


def params_for(mib):
    return pltpu.CompilerParams(vmem_limit_bytes=mib * 1024 * 1024)


def local(grads, owners, local_ids, params, first_moment, second_moment, step_count):
    groups = lax.axis_size("rows")
    slices = lax.axis_size("cols")
    count, width = grads.shape
    own, lanes = params.shape
    cap = max(2, 2 * count // groups)
    block = cap // 2 + 1
    peers = groups * slices
    message, select = pl.pallas_call(
        functools.partial(pack_kernel, groups, cap),
        out_shape=(
            jax.ShapeDtypeStruct((peers * block, lanes), jnp.int32),
            jax.ShapeDtypeStruct((count, groups * cap), jnp.bfloat16),
        ),
        in_specs=[HBM, HBM, HBM],
        out_specs=(HBM, HBM),
        scratch_shapes=[
            pltpu.VMEM((1, count), jnp.int32),
            pltpu.VMEM((1, count), jnp.int32),
            pltpu.VMEM((count, width), jnp.float32),
            pltpu.VMEM((peers * block + SPARE, lanes), jnp.int32),
            pltpu.VMEM((count, groups * cap), jnp.bfloat16),
            pltpu.SemaphoreType.DMA((2,)),
            pltpu.SemaphoreType.DMA,
            pltpu.SemaphoreType.DMA((slices,)),
            pltpu.SemaphoreType.DMA,
        ],
        compiler_params=params_for(56),
        name="pack",
    )(owners.reshape(1, count), local_ids.reshape(1, count), grads)
    message = message.reshape(peers, 1, block * lanes)
    message = lax.all_to_all(message, ORDER, split_axis=0, concat_axis=0, tiled=True)
    message = message.reshape(peers * block, lanes)
    table = jax.ShapeDtypeStruct((own, lanes), jnp.float32)
    new_params, new_first, new_second, answer = pl.pallas_call(
        functools.partial(update_kernel, cap),
        out_shape=(table, table, table, jax.ShapeDtypeStruct((peers * cap, lanes), jnp.bfloat16)),
        in_specs=[VMEM, VMEM, VMEM, VMEM, VMEM],
        out_specs=(HBM, HBM, HBM, VMEM),
        scratch_shapes=[
            pltpu.VMEM((SPARE * block + SPARE, lanes), jnp.int32),
            pltpu.VMEM((peers, lanes), jnp.int32),
            pltpu.VMEM((peers * cap // 2 + SPARE, lanes), jnp.float32),
            pltpu.VMEM((own // 2, 2 * lanes), jnp.bfloat16),
            pltpu.VMEM((3, own, lanes), jnp.float32),
            pltpu.SemaphoreType.DMA((3,)),
        ],
        compiler_params=params_for(48),
        name="update",
    )(message, step_count.reshape(1, 1), params, first_moment, second_moment)
    answer = answer.reshape(peers, cap, lanes)
    answer = lax.all_to_all(answer, ORDER, split_axis=0, concat_axis=0, tiled=True)
    row_steps = pl.pallas_call(
        unpack_kernel,
        out_shape=jax.ShapeDtypeStruct((count, width), jnp.bfloat16),
        in_specs=[VMEM, VMEM],
        out_specs=HBM,
        scratch_shapes=[pltpu.VMEM((count, width), jnp.bfloat16), pltpu.SemaphoreType.DMA((slices // 2,))],
        compiler_params=params_for(40),
        name="unpack",
    )(select, answer.reshape(peers * cap, lanes))
    return (new_params, new_first, new_second, row_steps)


def solution(mesh):
    placed = (
        P(("rows", "cols"), None),
        P(("rows", "cols"), None),
        P(("rows", "cols")),
        P("rows", "cols"),
        P("rows", "cols"),
        P("rows", "cols"),
        P(),
    )
    return jax.shard_map(
        local,
        mesh=mesh,
        in_specs=placed,
        out_specs=(
            P("rows", "cols"),
            P("rows", "cols"),
            P("rows", "cols"),
            P(("rows", "cols"), None),
        ),
        check_vma=False,
    )
```

```python
import functools

import jax
import jax.numpy as jnp
import numpy as np
from jax import lax
from jax.experimental import pallas as pl
from jax.experimental.pallas import tpu as pltpu
from jax.sharding import PartitionSpec as P

LANES = 128
FULL = 32767.0
TINY = 1e-30
SPARE = 8
ORDER = ("cols", "rows")


def iota(shape, axis):
    return lax.broadcasted_iota(jnp.int32, shape, axis)


def dot(a, b):
    return jnp.dot(a, b, preferred_element_type=jnp.float32)


def dot_nt(a, b):
    return lax.dot_general(a, b, (((1,), (1,)), ((), ())), preferred_element_type=jnp.float32)


def one_minus_power(base, steps):
    factor = 1.0 - float(np.float32(base))
    total = jnp.zeros_like(steps, jnp.float32)
    for bit in range(5):
        has = ((steps >> bit) & 1).astype(jnp.float32)
        total = total + has * np.float32(factor) * (1.0 - total)
        factor = factor * (2.0 - factor)
    return total


def pack_kernel(
    groups, cap, owners_hbm, ids_hbm, grads_hbm, message_hbm, select_hbm,
    owners_ref, ids_ref, grads_ref, message_ref, select_ref, names_sem, grads_sem, message_sem, select_sem,
):
    count, width = grads_ref.shape
    words = cap // 2
    block = words + 1
    slices = width // LANES
    share = groups * block
    names = [
        pltpu.make_async_copy(owners_hbm, owners_ref, names_sem.at[0]),
        pltpu.make_async_copy(ids_hbm, ids_ref, names_sem.at[1]),
    ]
    load = pltpu.make_async_copy(grads_hbm, grads_ref, grads_sem)
    for copy in names:
        copy.start()
    load.start()
    for copy in names:
        copy.wait()

    owner = owners_ref[...]
    mine = owner == iota((groups, count), 0)
    mine_half = mine.astype(jnp.bfloat16)
    square = (count, count)
    earlier = (iota(square, 0) < iota(square, 1)).astype(jnp.bfloat16)
    before = jnp.where(mine, dot(mine_half, earlier), 0.0)
    position = jnp.sum(before, axis=0, keepdims=True).astype(jnp.int32)
    place = (iota((groups * cap, count), 0) == position * groups + owner).astype(jnp.bfloat16)
    on_diagonal = iota(square, 0) == iota(square, 1)

    target = (owner * cap + position).astype(jnp.float32)
    target = jnp.sum(jnp.where(on_diagonal, target, 0.0), axis=1, keepdims=True).astype(jnp.int32)
    select_ref[...] = (iota((count, groups * cap), 1) == target).astype(jnp.bfloat16)
    stores = [pltpu.make_async_copy(select_ref, select_hbm, select_sem)]
    stores[0].start()

    named = ids_ref[...] + 1
    lane = iota((LANES, count), 0)
    at_id = lane == position
    at_power = lane == position + cap
    names_high = jnp.where(at_id, lax.div(named, 32).astype(jnp.float32), 0.0).astype(jnp.bfloat16)
    names_low = jnp.where(at_id, lax.rem(named, 32).astype(jnp.float32), 0.0).astype(jnp.bfloat16)
    facts = dot_nt(mine_half, names_high) * 32.0 + dot_nt(mine_half, names_low)

    load.wait()
    grads = grads_ref[...]
    size = jnp.abs(grads)
    top = jnp.max(size, axis=1, keepdims=True)
    power = jnp.ceil(jnp.log2(jnp.maximum(top, TINY)))
    code = jnp.minimum(jnp.floor(jnp.sqrt(size * jnp.exp2(-power)) * FULL + 0.5), FULL)
    code = jnp.where(grads < 0.0, -code, code)
    high = jnp.floor(code * (1.0 / 256.0) + 0.5)
    low = (code - high * 256.0).astype(jnp.bfloat16)
    high = high.astype(jnp.bfloat16)

    power_row = jnp.sum(jnp.where(on_diagonal, power, 0.0), axis=0, keepdims=True)
    powers = jnp.where(at_power, power_row, 0.0).astype(jnp.bfloat16)
    facts = (facts + dot_nt(mine_half, powers)).astype(jnp.int32)

    for c in range(slices):
        columns = slice(c * LANES, (c + 1) * LANES)
        placed = dot(place, jnp.concatenate([high[:, columns], low[:, columns]], axis=1))
        placed = (placed[:, :LANES] * 256.0 + placed[:, LANES:]).astype(jnp.int32)
        for j in range(words):
            one = placed[j * groups : (j + 1) * groups]
            two = placed[(j + words) * groups : (j + words + 1) * groups]
            message_ref[pl.ds(c * share + j, groups, stride=block), :] = (one & 0xFFFF) | (two << 16)
        message_ref[pl.ds(c * share + words, groups, stride=block), :] = facts
        rows = pl.ds(c * share, share)
        stores.append(pltpu.make_async_copy(message_ref.at[rows], message_hbm.at[rows], message_sem.at[c]))
        stores[-1].start()

    for copy in stores:
        copy.wait()


def update_kernel(
    cap, message_ref, step_ref, params_ref, first_ref, second_ref,
    new_params_hbm, new_first_hbm, new_second_hbm, answer_ref,
    tail_ref, facts_ref, spread_ref, halves_ref, table_ref, table_sem,
):
    own, lanes = params_ref.shape
    words = cap // 2
    block = words + 1
    sources = message_ref.shape[0] // block
    tail = SPARE * block
    tail_ref[:tail] = message_ref[sources * block - tail :]

    def row(j):
        most = message_ref[pl.ds(j, sources - SPARE, stride=block), :]
        return jnp.concatenate([most, tail_ref[pl.ds(j, SPARE, stride=block), :]], axis=0)

    facts = row(words)
    facts_ref[...] = facts
    across = facts.astype(jnp.float32).T
    id_rows = across[:cap].astype(jnp.int32) - 1
    scale_rows = jnp.exp2(across[cap : 2 * cap]).astype(jnp.bfloat16)
    short_rows = id_rows.astype(jnp.int16)
    fine = 32
    coarse = own // fine
    counts = jnp.zeros((coarse, fine), jnp.float32)
    for s in range(cap):
        ids = id_rows[s : s + 1]
        whole = (iota((coarse, sources), 0) == lax.div(ids, fine)).astype(jnp.bfloat16)
        rest = (iota((fine, sources), 0) == lax.rem(ids, fine)).astype(jnp.bfloat16)
        counts = counts + dot_nt(whole, rest)
    counts = jnp.minimum(counts, 1.0).astype(jnp.bfloat16)
    whole = (lax.div(iota((own, coarse), 0), fine) == iota((own, coarse), 1)).astype(jnp.bfloat16)
    rest = lax.rem(iota((own, fine), 0), fine) == iota((own, fine), 1)
    live = jnp.sum(jnp.where(rest, dot(whole, counts), 0.0), axis=1, keepdims=True) > 0.0
    items = iota((own, sources), 0).astype(jnp.int16)
    total = jnp.zeros((own, 2 * lanes), jnp.float32)
    for j in range(words):
        word = row(j)
        for s, code in ((j, (word << 16) >> 16), (j + words, word >> 16)):
            code = code.astype(jnp.float32)
            value = code * jnp.abs(code)
            high = value.astype(jnp.bfloat16)
            low = (value - high.astype(jnp.float32)).astype(jnp.bfloat16)
            hit = jnp.where(items == short_rows[s : s + 1], scale_rows[s : s + 1], jnp.bfloat16(0))
            total = total + dot(hit, jnp.concatenate([high, low], axis=1))
    summed = (total[:, :lanes] + total[:, lanes:]) * (1.0 / (FULL * FULL))
    fix_first = one_minus_power(0.9, step_ref[...])
    fix_second = one_minus_power(0.999, step_ref[...])
    first, second, params = first_ref[...], second_ref[...], params_ref[...]
    new_first = jnp.where(live, 0.9 * first + 0.1 * summed, first)
    new_second = jnp.where(live, 0.999 * second + 0.001 * summed * summed, second)
    direction = -(new_first * (1.0 / fix_first)) / (jnp.sqrt(new_second * (1.0 / fix_second)) + 1e-08)
    table_ref[0] = jnp.where(live, params + 0.01 * direction, params)
    table_ref[1] = new_first
    table_ref[2] = new_second
    copies = [
        pltpu.make_async_copy(table_ref.at[n], out, table_sem.at[n])
        for n, out in enumerate((new_params_hbm, new_first_hbm, new_second_hbm))
    ]
    for copy in copies:
        copy.start()

    half = own // 2
    direction = direction.astype(jnp.bfloat16)
    halves_ref[...] = jnp.concatenate([direction[:half], direction[half:]], axis=1)
    part = sources // 2
    spots = iota((cap * part, half), 1).astype(jnp.int16)

    def answer_part(p, carry):
        ids = facts_ref[pl.ds(pl.multiple_of(p * part, part), part), :] - 1
        wanted = jnp.concatenate([jnp.broadcast_to(ids[:, s : s + 1], (part, lanes)) for s in range(cap)], axis=0)
        upper = wanted >= half
        spot = jnp.where(upper, wanted - half, wanted).astype(jnp.int16)
        hit = jnp.where(spots == jnp.concatenate([spot] * (half // lanes), axis=1), jnp.bfloat16(1), jnp.bfloat16(0))
        both = dot(hit, halves_ref[...])
        found = jnp.where(upper, both[:, lanes:], both[:, :lanes])
        for s in range(cap):
            spread_ref[pl.ds(s, part, stride=cap), :] = found[s * part : (s + 1) * part]
        rows = pl.ds(pl.multiple_of(p * part * cap, part * cap), part * cap)
        answer_ref[rows, :] = spread_ref[: part * cap].astype(jnp.bfloat16)
        return carry

    lax.fori_loop(0, 2, answer_part, 0)
    for copy in copies:
        copy.wait()


def unpack_kernel(select_ref, back_ref, out_hbm, out_ref, out_sem):
    select = select_ref[...]
    slots = select.shape[1]
    copies = []
    for c in range(0, out_ref.shape[1] // LANES, 2):
        columns = pl.ds(c * LANES, 2 * LANES)
        one, two = back_ref[c * slots : (c + 1) * slots], back_ref[(c + 1) * slots : (c + 2) * slots]
        out_ref[:, columns] = dot(select, jnp.concatenate([one, two], axis=1)).astype(jnp.bfloat16)
        copies.append(pltpu.make_async_copy(out_ref.at[:, columns], out_hbm.at[:, columns], out_sem.at[c // 2]))
        copies[-1].start()
    for copy in copies:
        copy.wait()


VMEM = pl.BlockSpec(memory_space=pltpu.VMEM)
HBM = pl.BlockSpec(memory_space=pltpu.HBM)


def params_for(mib):
    return pltpu.CompilerParams(vmem_limit_bytes=mib * 1024 * 1024)


def local(grads, owners, local_ids, params, first_moment, second_moment, step_count):
    groups = lax.axis_size("rows")
    slices = lax.axis_size("cols")
    count, width = grads.shape
    own, lanes = params.shape
    cap = max(2, 2 * count // groups)
    block = cap // 2 + 1
    peers = groups * slices
    message, select = pl.pallas_call(
        functools.partial(pack_kernel, groups, cap),
        out_shape=(
            jax.ShapeDtypeStruct((peers * block, lanes), jnp.int32),
            jax.ShapeDtypeStruct((count, groups * cap), jnp.bfloat16),
        ),
        in_specs=[HBM, HBM, HBM],
        out_specs=(HBM, HBM),
        scratch_shapes=[
            pltpu.VMEM((1, count), jnp.int32),
            pltpu.VMEM((1, count), jnp.int32),
            pltpu.VMEM((count, width), jnp.float32),
            pltpu.VMEM((peers * block + SPARE, lanes), jnp.int32),
            pltpu.VMEM((count, groups * cap), jnp.bfloat16),
            pltpu.SemaphoreType.DMA((2,)),
            pltpu.SemaphoreType.DMA,
            pltpu.SemaphoreType.DMA((slices,)),
            pltpu.SemaphoreType.DMA,
        ],
        compiler_params=params_for(56),
        name="pack",
    )(owners.reshape(1, count), local_ids.reshape(1, count), grads)
    message = message.reshape(peers, 1, block * lanes)
    message = lax.all_to_all(message, ORDER, split_axis=0, concat_axis=0, tiled=True)
    message = message.reshape(peers * block, lanes)
    table = jax.ShapeDtypeStruct((own, lanes), jnp.float32)
    new_params, new_first, new_second, answer = pl.pallas_call(
        functools.partial(update_kernel, cap),
        out_shape=(table, table, table, jax.ShapeDtypeStruct((peers * cap, lanes), jnp.bfloat16)),
        in_specs=[VMEM, VMEM, VMEM, VMEM, VMEM],
        out_specs=(HBM, HBM, HBM, VMEM),
        scratch_shapes=[
            pltpu.VMEM((SPARE * block + SPARE, lanes), jnp.int32),
            pltpu.VMEM((peers, lanes), jnp.int32),
            pltpu.VMEM((peers * cap // 2 + SPARE, lanes), jnp.float32),
            pltpu.VMEM((own // 2, 2 * lanes), jnp.bfloat16),
            pltpu.VMEM((3, own, lanes), jnp.float32),
            pltpu.SemaphoreType.DMA((3,)),
        ],
        compiler_params=params_for(48),
        name="update",
    )(message, step_count.reshape(1, 1), params, first_moment, second_moment)
    answer = answer.reshape(peers, cap, lanes)
    answer = lax.all_to_all(answer, ORDER, split_axis=0, concat_axis=0, tiled=True)
    row_steps = pl.pallas_call(
        unpack_kernel,
        out_shape=jax.ShapeDtypeStruct((count, width), jnp.bfloat16),
        in_specs=[VMEM, VMEM],
        out_specs=HBM,
        scratch_shapes=[pltpu.VMEM((count, width), jnp.bfloat16), pltpu.SemaphoreType.DMA((slices // 2,))],
        compiler_params=params_for(40),
        name="unpack",
    )(select, answer.reshape(peers * cap, lanes))
    return (new_params, new_first, new_second, row_steps)


def solution(mesh):
    placed = (
        P(("rows", "cols"), None),
        P(("rows", "cols"), None),
        P(("rows", "cols")),
        P("rows", "cols"),
        P("rows", "cols"),
        P("rows", "cols"),
        P(),
    )
    return jax.shard_map(
        local,
        mesh=mesh,
        in_specs=placed,
        out_specs=(
            P("rows", "cols"),
            P("rows", "cols"),
            P("rows", "cols"),
            P(("rows", "cols"), None),
        ),
        check_vma=False,
    )
```
